128 devices in a mesh: dp: 16 (over z, x_lo, core), seq: 8 (over x_hi, y).
Axes of the slice: x: 4 (x_hi: 2, x_lo: 2; x = x_hi * 2 + x_lo), y: 4, z: 4, core: 2. Of those that a mesh axis runs over, the one named last changes fastest.
Arguments:
- inputs: bfloat16 [16, 1024, 1024], P('dp', 'seq'), may hold values from -6 to 6
- doc_ids: int32 [16, 1024], P('dp', 'seq'), may hold values from 0 to 2, as said below
- w_query: bfloat16 [1024, 1024], P('dp'), may hold values from -0.1875 to 0.1875
- w_key: bfloat16 [1024, 512], P('dp'), may hold values from -0.1875 to 0.1875
- w_value: bfloat16 [1024, 512], P('dp'), may hold values from -0.1875 to 0.1875
- w_out: bfloat16 [1024, 1024], P('dp'), may hold values from -0.75 to 0.75
- w_gate: bfloat16 [1024, 4608], P('dp'), may hold values from -0.1875 to 0.1875
- w_up: bfloat16 [1024, 4608], P('dp'), may hold values from -0.1875 to 0.1875
- w_down: bfloat16 [4608, 1024], P('dp'), may hold values from -0.09375 to 0.09375
- attn_gain: bfloat16 [1024], P('dp'), may hold values from 0.099609375 to 1.8984375
- ffn_gain: bfloat16 [1024], P('dp'), may hold values from 0.099609375 to 1.8984375
- query_gain: bfloat16 [64], P('dp'), may hold values from 0.099609375 to 1.8984375
- key_gain: bfloat16 [64], P('dp'), may hold values from 0.099609375 to 1.8984375
- cotangent: bfloat16 [16, 1024, 1024], P('dp', 'seq'), may hold values from -6 to 6
Outputs:
- block_out: bfloat16 [16, 1024, 1024], P('dp', 'seq')
- grad_inputs: float32 [16, 1024, 1024], P('dp', 'seq')
- grad_query: float32 [1024, 1024], P('dp')
- grad_key: float32 [1024, 512], P('dp')
- grad_value: float32 [1024, 512], P('dp')
- grad_out: float32 [1024, 1024], P('dp')
- grad_gate: float32 [1024, 4608], P('dp')
- grad_up: float32 [1024, 4608], P('dp')
- grad_down: float32 [4608, 1024], P('dp')
- grad_attn_gain: float32 [1024], P('dp')
- grad_ffn_gain: float32 [1024], P('dp')
- grad_query_gain: float32 [64], P('dp')
- grad_key_gain: float32 [64], P('dp')
The draws below stay inside these ranges and needn't reach their ends.
Inputs may be any that keep to these rules, and one draw needn't show every extreme that they name: `doc_ids`: every sequence holds three documents numbered 0, 1, 2 in order; document 0 ends within the first 128 tokens and document 2 begins within the last 128 tokens.
All inputs are finite; a program needn't handle non-finite values.
Results may differ from the reference program's by a relative error of at most 0.028.
Values may be sent and summed in bfloat16 or wider, within the bound.
No kernel may reach another device: no remote copies, remote signals or barrier semaphores. Data moves between devices by JAX's collectives and lax.ppermute only.
A program may use at most 192 MiB of HBM per device.

```python
import jax
import jax.numpy as jnp
from jax import lax

D = 1024
FF = 4608
H = 16
KV = 8
HD = 64
LENGTH = 1024
SEQUENCES = 16
ROWS = 128


def draw_doc_ids(key, part):
    key = jax.random.fold_in(key, 11)
    first_key, second_key = jax.random.split(key)
    first_cut = jax.random.randint(first_key, (SEQUENCES, 1), 1, ROWS)
    second_cut = jax.random.randint(second_key, (SEQUENCES, 1), LENGTH - ROWS + 1, LENGTH)
    places = jnp.arange(LENGTH, dtype=jnp.int32)[None, :]
    return ((places >= first_cut).astype(jnp.int32) + (places >= second_cut).astype(jnp.int32)).astype(jnp.int32)


def steps_of(own_key, dims, pieces, smallest, largest):
    level, own = 1.0, jax.random.fold_in(own_key, 6)
    for axis_at, shards_of in pieces:
        draws = jnp.exp(jax.random.uniform(jax.random.fold_in(own, axis_at), (shards_of,), jnp.float32, smallest / len(pieces), largest / len(pieces)))
        level = level * jnp.repeat(draws, dims[axis_at] // shards_of).reshape([-1 if axis == axis_at else 1 for axis in range(len(dims))])
    return level


def gaussian(stream_key, shape, spread, bound, cuts=(), kind=jnp.bfloat16):
    loudness = steps_of(stream_key, shape, cuts, -0.22, 0.18) if cuts else 1.0
    array = jax.random.normal(stream_key, shape, jnp.float32) * spread * loudness
    return jnp.minimum(jnp.maximum(array, -bound), bound).astype(kind)


def setup_inputs(seed: int = 0) -> dict:
    splits = jax.random.split(jax.random.key(seed), 15)
    return {
        "inputs": gaussian(splits[0], (SEQUENCES, LENGTH, D), 1.0, 6.0, ((0, 16), (1, 8))),
        "doc_ids": draw_doc_ids(jax.random.fold_in(splits[14], 71), 0),
        "w_query": gaussian(splits[2], (D, H * HD), D ** -0.5, 0.1875, ((0, 16),)),
        "w_key": gaussian(splits[3], (D, KV * HD), D ** -0.5, 0.1875, ((0, 16),)),
        "w_value": gaussian(splits[4], (D, KV * HD), D ** -0.5, 0.1875, ((0, 16),)),
        "w_out": gaussian(splits[5], (H * HD, D), (H * HD // 16) ** -0.5, 0.75, ((0, 16),)),
        "w_gate": gaussian(splits[6], (D, FF), D ** -0.5, 0.1875, ((0, 16),)),
        "w_up": gaussian(splits[7], (D, FF), D ** -0.5, 0.1875, ((0, 16),)),
        "w_down": gaussian(splits[8], (FF, D), FF ** -0.5, 0.09375, ((0, 16),)),
        "attn_gain": jnp.clip(1.0 + 0.18 * jax.random.normal(splits[9], (D,), jnp.float32), 0.099609375, 1.8984375).astype(jnp.bfloat16),
        "ffn_gain": jnp.clip(1.0 + 0.18 * jax.random.normal(splits[10], (D,), jnp.float32), 0.099609375, 1.8984375).astype(jnp.bfloat16),
        "query_gain": jnp.clip(1.0 + 0.18 * jax.random.normal(splits[11], (HD,), jnp.float32), 0.099609375, 1.8984375).astype(jnp.bfloat16),
        "key_gain": jnp.clip(1.0 + 0.18 * jax.random.normal(splits[12], (HD,), jnp.float32), 0.099609375, 1.8984375).astype(jnp.bfloat16),
        "cotangent": gaussian(splits[13], (SEQUENCES, LENGTH, D), 1.0, 6.0, ((0, 16), (1, 8))),
    }


EPS = 1e-05
BASE = 1000000.0
MASKED = -1e+30

@jax.custom_vjp
def low(v):
    return lax.optimization_barrier(v.astype(jnp.bfloat16)).astype(jnp.float32)

@jax.custom_vjp
def low_back(v):
    return v

def low_keep(v):
    return (low(v), None)

def low_pass(kept, grad):
    return (grad,)

def back_keep(v):
    return (v, None)

def back_low(kept, grad):
    return (low(grad),)
low.defvjp(low_keep, low_pass)
low_back.defvjp(back_keep, back_low)

def matmul_high(left, right):
    return jnp.dot(left, right, precision=lax.Precision.HIGHEST, preferred_element_type=jnp.float32)

def rms_norm(values, gain):
    return values * lax.rsqrt(lax.optimization_barrier(jnp.mean(values * values, axis=-1, keepdims=True)) + EPS) * gain

def doc_positions(ids):
    places = jnp.arange(ids.shape[0], dtype=jnp.int32)
    first = jnp.concatenate([jnp.ones((1,), dtype=bool), ids[1:] != ids[:-1]])
    starts = lax.cummax(jnp.where(first, places, 0), axis=0)
    return places - starts

def rope_tables(positions):
    half_width = HD // 2
    freqs = BASE ** (-(jnp.arange(half_width, dtype=jnp.float32) * (2.0 / HD)))
    angles = positions.astype(jnp.float32)[:, None] * freqs[None, :]
    return (jnp.cos(angles)[:, None, :], jnp.sin(angles)[:, None, :])

def rotate(values, cosine, sine):
    half_width = HD // 2
    first_half = values[..., :half_width]
    second_half = values[..., half_width:]
    return jnp.concatenate([first_half * cosine - second_half * sine, second_half * cosine + first_half * sine], axis=-1)

def forward(states, ids, wq, wk, wv, wo, wg, wu, wd, g_attn, g_ffn, g_query, g_key):
    seq_len = states.shape[0]
    group = H // KV
    places = jnp.arange(seq_len, dtype=jnp.int32)
    cosine, sine = rope_tables(doc_positions(ids))
    normed = low(rms_norm(states, g_attn))
    query = low_back(matmul_high(normed, wq)).reshape(seq_len, H, HD)
    key = low_back(matmul_high(normed, wk)).reshape(seq_len, KV, HD)
    value = low_back(low(matmul_high(normed, wv))).reshape(seq_len, KV, HD)
    query = low_back(low(rotate(rms_norm(query, g_query), cosine, sine)))
    key = low_back(low(rotate(rms_norm(key, g_key), cosine, sine)))
    block_rows = min(512, seq_len)
    blocks_count = seq_len // block_rows
    scale = HD ** (-0.5)
    query_blocks = query.reshape(blocks_count, block_rows, KV, group, HD)

    def one_block(block_args):
        query_part, block_index = block_args
        start = block_index * block_rows
        query_places = start + jnp.arange(block_rows, dtype=jnp.int32)
        query_ids = lax.dynamic_slice_in_dim(ids, start, block_rows)
        scores = jnp.einsum('qkgd,tkd->kgqt', query_part, key, precision=lax.Precision.HIGHEST) * scale
        scores = low_back(scores)
        allowed = (ids[None, :] == query_ids[:, None]) & (places[None, :] <= query_places[:, None])
        scores = jnp.where(allowed, scores, MASKED)
        top = lax.optimization_barrier(jnp.max(scores, axis=-1, keepdims=True))
        expd = jnp.exp(scores - top)
        probs = low(expd / lax.optimization_barrier(jnp.sum(expd, axis=-1, keepdims=True)))
        mixed = jnp.einsum('kgqt,tkd->qkgd', probs, value, precision=lax.Precision.HIGHEST)
        return mixed.reshape(block_rows, H * HD)
    attended = lax.map(jax.checkpoint(one_block), (query_blocks, jnp.arange(blocks_count, dtype=jnp.int32)))
    attended = low_back(low(attended.reshape(seq_len, H * HD)))
    resid = states + low_back(matmul_high(attended, wo))
    normed2 = low(rms_norm(resid, g_ffn))
    gate = low_back(matmul_high(normed2, wg))
    upper = low_back(matmul_high(normed2, wu))
    hidden = low(jax.nn.silu(gate) * upper)
    return resid + matmul_high(hidden, wd)

def reference(inputs, doc_ids, w_query, w_key, w_value, w_out, w_gate, w_up, w_down, attn_gain, ffn_gain, query_gain, key_gain, cotangent):
    weights = tuple((item.astype(jnp.float32) for item in (w_query, w_key, w_value, w_out, w_gate, w_up, w_down, attn_gain, ffn_gain, query_gain, key_gain)))

    def one_sequence(carry, item):
        states, ids, cot = item

        def local_forward(states_in, *params):
            return forward(states_in, ids, *params)
        output, pull = jax.vjp(local_forward, states.astype(jnp.float32), *weights)
        grads = pull(cot.astype(jnp.float32))
        totals = tuple((total + grad for total, grad in zip(carry, grads[1:])))
        return (totals, (output.astype(jnp.bfloat16), grads[0]))
    start = tuple((jnp.zeros(item.shape, jnp.float32) for item in weights))
    totals, (outputs, grad_states) = lax.scan(one_sequence, start, (inputs, doc_ids, cotangent))
    return (outputs, grad_states, totals[0], totals[1], totals[2], totals[3], totals[4], totals[5], totals[6], totals[7], totals[8], totals[9], totals[10])
```

```python
import functools

import jax
import jax.numpy as jnp
from jax import lax
from jax.experimental import pallas as pl
from jax.experimental.pallas import tpu as pltpu
from jax.sharding import PartitionSpec as P

H = 16
KV = 8
HD = 64
SIDE = 4

EPS = 1e-05
BASE = 1000000.0
MASKED = -1e30
SCALE = HD ** (-0.5)
BF16 = jnp.bfloat16
F32 = jnp.float32
VMEM_LIMIT = 50 * 1024 * 1024


def left_dot(left, right):
    return lax.dot_general(left, right, (((0,), (0,)), ((), ())), preferred_element_type=F32)


def right_dot(left, right):
    return lax.dot_general(left, right, (((1,), (1,)), ((), ())), preferred_element_type=F32)


def dot(left, right):
    return lax.dot_general(left, right, (((1,), (0,)), ((), ())), preferred_element_type=F32)


def norm_parts(values):
    inverse = lax.rsqrt(jnp.mean(values * values, axis=-1, keepdims=True) + EPS)
    return (values * inverse, inverse)


def norm_back(incoming, normal, inverse):
    return inverse * (incoming - normal * jnp.mean(incoming * normal, axis=-1, keepdims=True))


def swap(block, axis, step):
    size = lax.axis_size(axis)
    return lax.ppermute(block, axis, [(i, i ^ step) for i in range(size)])


def gather_side(block):
    return [block] + [swap(block, "seq", k) for k in range(1, SIDE)]


def scatter_side(blocks):
    return [blocks[0]] + [swap(blocks[k], "seq", k) for k in range(1, SIDE)]


def tie(value, *after):
    return lax.optimization_barrier((value,) + after)[0]


def take(array, index, axis):
    return lax.dynamic_index_in_dim(array, index, axis=axis, keepdims=False)


def added(*pieces):
    return sum(piece.astype(F32) for piece in pieces).astype(BF16)


def send_along_z(total, mine):
    z = mine // 4
    return [take(total, z, 0)] + [swap(take(total, z ^ k, 0), "dp", 4 * k) for k in range(1, 4)]


def whole(count):
    return [pl.BlockSpec(memory_space=pltpu.VMEM)] * count


def lanes(shape):
    return lax.broadcasted_iota(jnp.int32, shape, len(shape) - 1)


def head_mean(values):
    row = lax.broadcasted_iota(jnp.int32, (128, 128), 0)
    ones = jnp.where(row // HD == lanes((128, 128)) // HD, 1.0 / HD, 0.0).astype(BF16)
    high = values.astype(BF16)
    rest = (values - high.astype(F32)).astype(BF16)
    return dot(high, ones) + dot(rest, ones)


def partner(values):
    return jnp.where(
        lanes(values.shape) % HD < HD // 2,
        pltpu.roll(values, 128 - HD // 2, 1),
        pltpu.roll(values, HD // 2, 1),
    )


def doubled(pair, head):
    other = pltpu.roll(pair.astype(F32), HD, 1).astype(pair.dtype)
    first = lanes(pair.shape) < HD
    return jnp.where(first, pair, other) if head == 0 else jnp.where(first, other, pair)


def two_heads(block):
    first = lanes(block.shape) < HD
    zero = jnp.zeros_like(block)
    return jnp.concatenate([jnp.where(first, block, zero), jnp.where(first, zero, block)], axis=0)


def sublanes(shape):
    return lax.broadcasted_iota(jnp.int32, shape, len(shape) - 2)


def pack_kernel(few, where, query, key, value, out_weight, gains, pack, scratch, sems):
    side, mine = where[0], where[1]
    shard, width = out_weight.shape
    copies = []
    begin = 0
    for weight in (query, key, value):
        count = weight.shape[1] // SIDE
        at = pl.ds(pl.multiple_of(side * count, count), count)
        copies.append((weight.at[:, at], pack.at[pl.ds(0, shard), pl.ds(begin, count)]))
        begin += count
    copies.append((out_weight, pack.at[pl.ds(0, shard), pl.ds(begin, width)]))
    copies = [
        pltpu.make_async_copy(source, target, sems.at[index])
        for index, (source, target) in enumerate(copies)
    ]
    for copy in copies:
        copy.start()

    def spread(gain, count, lane_count):
        row = jnp.concatenate([gain] * (lane_count // count), axis=1)
        return row, lanes(row.shape)

    all_gains = gains[...].astype(F32)
    rows = []
    for gain in (all_gains[:, :shard], all_gains[:, shard : 2 * shard]):
        row, lane = spread(gain, shard, width)
        rows.append(jnp.where(lane // shard == mine, row, 0.0))
    for index in range(2):
        gain = all_gains[:, 2 * shard + index * few : 2 * shard + (index + 1) * few]
        row, lane = spread(gain, few, 128)
        row = jnp.where(lane % HD // few == mine, row, 0.0)
        rows.append(jnp.concatenate([row, jnp.zeros((1, width - 128), F32)], axis=1))
    at = sublanes((16, width))
    extra = jnp.zeros((16, width), F32)
    for index, row in enumerate(rows):
        extra = jnp.where(at == index, row, extra)
    extra = jnp.concatenate([extra, jnp.zeros((16, begin), F32)], axis=1)
    scratch[...] = extra.astype(BF16)
    last = pltpu.make_async_copy(scratch, pack.at[pl.ds(shard, 16), :], sems.at[len(copies)])
    last.start()
    for copy in copies + [last]:
        copy.wait()


def start_of(place, cuts):
    return jnp.where(place >= cuts[1], cuts[1], jnp.where(place >= cuts[0], cuts[0], 0.0))


def forward_kernel(parts, me, *refs):
    token_refs = refs[:parts]
    packed, cos_table, sin_table = refs[parts : parts + 3]
    normed_out, q_raw, k_raw, query, key, value, mixed, gains = refs[parts + 3 : parts + 11]
    cosine, sine, bounds, k_two, v_two = refs[parts + 11 :]
    rows = query.shape[0] // SIDE
    width = token_refs[0].shape[1]
    q_cols = query.shape[1]
    cols = q_cols + 2 * key.shape[1]
    shard = packed.shape[1] - 16
    weight = packed[:, :shard, :cols].reshape(width, cols)
    gains[...] = jnp.sum(packed[:, shard:, :width].astype(F32), axis=0)
    gain, q_gain, k_gain = gains[0:1, :], gains[2:3, :128], gains[3:4, :128]

    bases = [(me[0] ^ part) * rows for part in range(parts)]
    row_places = [(lanes((1, rows)) + base).astype(F32) for base in bases]
    cuts = []
    for number in (1.0, 2.0):
        least = jnp.full((1, rows), 4096.0, F32)
        for part in range(parts):
            ids = token_refs[part][rows:, :rows].astype(F32)[0:1]
            least = jnp.minimum(least, jnp.where(ids == number, row_places[part], 4096.0))
        cuts.append(jnp.min(least, axis=1, keepdims=True))
    for index in range(2):
        bounds[index : index + 1, :] = jnp.broadcast_to(cuts[index], (1, 128))
    at_cut = []
    all_places = sublanes(cos_table.shape).astype(F32)
    for cut in cuts:
        there = all_places == cut
        at_cut.append(
            [
                jnp.sum(jnp.where(there, table[...], 0.0), axis=0, keepdims=True)
                for table in (cos_table, sin_table)
            ]
        )
    sign = jnp.where(lanes((1, 128)) % HD < HD // 2, -1.0, 1.0)

    for part in range(parts):
        at = pl.ds(part * rows, rows)
        states = token_refs[part][:rows, :].astype(F32)
        inverse = lax.rsqrt(jnp.mean(states * states, axis=-1, keepdims=True) + EPS)
        normed = (states * inverse * gain).astype(BF16)
        there = pl.ds(pl.multiple_of(bases[part], rows), rows)
        place = (sublanes((rows, 128)) + bases[part]).astype(F32)
        cos_cut = jnp.where(
            place >= cuts[1], at_cut[1][0], jnp.where(place >= cuts[0], at_cut[0][0], 1.0)
        )
        sin_cut = jnp.where(
            place >= cuts[1], at_cut[1][1], jnp.where(place >= cuts[0], at_cut[0][1], 0.0)
        )
        cos = cos_table[there, :] * cos_cut + sin_table[there, :] * sin_cut
        sin = (sin_table[there, :] * cos_cut - cos_table[there, :] * sin_cut) * sign
        cosine[at, :] = cos
        sine[at, :] = sin
        normed_out[at, :] = normed
        if part < SIDE:
            raw = dot(normed, weight)
            raw_q, raw_kv = raw[:, :q_cols], raw[:, q_cols:]
            q_raw[at, :] = raw_q
            for pair in range(q_cols // 128):
                here = pl.ds(pair * 128, 128)
                one = raw_q[:, pair * 128 : (pair + 1) * 128]
                scaled = one * lax.rsqrt(head_mean(one * one) + EPS) * q_gain
                query[at, here] = (scaled * cos + partner(scaled) * sin).astype(BF16)
        else:
            raw_kv = dot(normed, weight[:, q_cols:])
        one = raw_kv[:, :128]
        k_raw[at, :] = one
        scaled = one * lax.rsqrt(head_mean(one * one) + EPS) * k_gain
        key[at, :] = (scaled * cos + partner(scaled) * sin).astype(BF16)
        value[at, :] = raw_kv[:, 128:].astype(BF16)
    k_place = jnp.concatenate(row_places, axis=1)
    for pair in range(q_cols // 128):
        here = pl.ds(pair * 128, 128)
        k_two[...] = doubled(key[...], pair)
        v_two[...] = doubled(value[...], pair)

        @pl.loop(0, SIDE)
        def _(step):
            at = pl.ds(pl.multiple_of(step * rows, rows), rows)
            q_place = (sublanes((rows, 1)) + (me[0] ^ step) * rows).astype(F32)
            q_place = jnp.concatenate([q_place, q_place], axis=0)
            allowed = (k_place <= q_place) & (k_place >= start_of(q_place, cuts))
            scores = right_dot(two_heads(query[at, here]), k_two[...]) * SCALE
            scores = jnp.where(allowed, scores, MASKED)
            expd = jnp.exp(scores - jnp.max(scores, axis=-1, keepdims=True))
            probs = (expd * (1.0 / jnp.sum(expd, axis=-1, keepdims=True))).astype(BF16)
            both = dot(probs, v_two[...])
            mixed[at, here] = jnp.where(
                lanes((rows, 128)) < HD, both[:rows], both[rows:]
            ).astype(BF16)


def backward_kernel(me, *refs):
    d_mixed, attended = refs[:SIDE], refs[SIDE : 2 * SIDE]
    query, key, value, q_raw, k_raw, cosine, sine, normed = refs[2 * SIDE : 2 * SIDE + 8]
    gains, bounds, d_q_raw, d_kv_raw, keep, send = refs[2 * SIDE + 8 : 2 * SIDE + 14]
    k_two, v_two, d_k, d_v, d_q, d_both, k_place, all_attended, d_cols = refs[2 * SIDE + 14 :]
    rows = d_mixed[0].shape[0]
    length = key.shape[0]
    q_cols = query.shape[1]
    pairs = q_cols // 128
    q_gain, k_gain = gains[2:3, :128], gains[3:4, :128]
    cuts = [bounds[0:1, :], bounds[1:2, :]]
    for part in range(SIDE):
        at = pl.ds(part * rows, rows)
        d_both[at, :] = d_mixed[part][:, :q_cols]
        d_cols[at, :] = d_mixed[part][:, q_cols:]
        all_attended[at, :] = attended[part][...]
    for part in range(length // rows):
        base = (me[0] ^ part) * rows
        k_place[pl.ds(part * rows, rows), :] = (sublanes((rows, 128)) + base).astype(F32)
    for pair in range(pairs):
        here = pl.ds(pair * 128, 128)
        k_two[...] = doubled(key[...], pair)
        v_two[...] = doubled(value[...], pair)
        d_k[pair] = jnp.zeros((length, 128), F32)
        d_v[pair] = jnp.zeros((length, 128), F32)

        @pl.loop(0, SIDE)
        def _(step):
            at = pl.ds(pl.multiple_of(step * rows, rows), rows)
            q_place = (lanes((1, rows)) + (me[0] ^ step) * rows).astype(F32)
            allowed = (k_place[...] <= q_place) & (k_place[...] >= start_of(q_place, cuts))
            allowed = jnp.concatenate([allowed, allowed], axis=1)
            q_two = two_heads(query[at, here])
            d_two = two_heads(d_both[at, here])
            scores = jnp.where(allowed, right_dot(k_two[...], q_two) * SCALE, MASKED)
            expd = jnp.exp(scores - jnp.max(scores, axis=0, keepdims=True))
            probs = expd * (1.0 / jnp.sum(expd, axis=0, keepdims=True))
            d_probs = right_dot(v_two[...], d_two)
            delta = jnp.sum(probs * d_probs, axis=0, keepdims=True)
            d_scores = (probs * (d_probs - delta)).astype(BF16)
            d_v[pair] += dot(probs.astype(BF16), d_two)
            d_k[pair] += dot(d_scores, q_two)
            both = left_dot(d_scores, k_two[...])
            d_q[at, here] = jnp.where(lanes((rows, 128)) < HD, both[:rows], both[rows:]) * SCALE

    first = lanes((rows, 128)) < HD
    sums = [jnp.zeros((1, 128), F32), jnp.zeros((1, 128), F32)]

    def back(incoming, raw, gain, at, which):
        inverse = lax.rsqrt(head_mean(raw * raw) + EPS)
        normal = raw * inverse
        incoming = incoming.astype(BF16).astype(F32)
        turned = incoming * cosine[at, :] - partner(incoming) * sine[at, :]
        sums[which] = sums[which] + jnp.sum(turned * normal, axis=0, keepdims=True)
        turned = turned * gain
        return (inverse * (turned - normal * head_mean(turned * normal))).astype(BF16)

    def joined(pieces):
        pieces = [piece + pltpu.roll(piece, HD, 1) for piece in pieces]
        return jnp.where(first, pieces[0], pieces[1])

    for part in range(length // rows):
        at = pl.ds(part * rows, rows)
        if part < SIDE:
            for pair in range(pairs):
                here = pl.ds(pair * 128, 128)
                d_q_raw[at, here] = back(d_q[at, here], q_raw[at, here], q_gain, at, 0)
        d_key = joined([d_k[pair, at, :] for pair in range(pairs)]) * SCALE
        d_kv_raw[at, :128] = back(d_key, k_raw[at, :], k_gain, at, 1)
        d_kv_raw[at, 128:] = joined([d_v[pair, at, :] for pair in range(pairs)]).astype(BF16)

    half = SIDE * rows
    width = normed.shape[1]
    shard = HD
    few = HD * shard // width
    sums = [total + pltpu.roll(total, HD, 1) for total in sums]
    row, lane = sublanes((8, 128)), lanes((8, 128))

    def gain_block(p):
        there = (row < few) & (lane == p * few + row)
        sides = [jnp.sum(jnp.where(there, total, 0.0), axis=1, keepdims=True) for total in sums]
        block = jnp.where(lane == 0, sides[0], jnp.where(lane == 1, sides[1], 0.0))
        return jnp.concatenate([block, jnp.zeros((shard - 8, 128), F32)], axis=0)

    first_core = me[1] == 0
    for chunk in range(width // 256):
        here = pl.ds(chunk * 256, 256)
        terms = jnp.concatenate(
            [
                left_dot(normed[:half, here], d_q_raw[...]),
                left_dot(normed[:, here], d_kv_raw[...]),
                left_dot(all_attended[:, here], d_cols[...]),
            ],
            axis=1,
        )
        for pair in range(256 // (2 * shard)):
            blocks = []
            for core in range(2):
                begin = (2 * pair + core) * shard
                p = begin // shard + chunk * (256 // shard)
                blocks.append(
                    jnp.concatenate([terms[begin : begin + shard], gain_block(p)], axis=1)
                )
            at = pl.ds((chunk * (256 // shard) // 2 + pair) * shard, shard)
            keep[at, :] = jnp.where(first_core, blocks[0], blocks[1]).astype(BF16)
            send[at, :] = jnp.where(first_core, blocks[1], blocks[0]).astype(BF16)


def terms_kernel(where, tokens, d_gate_up, hidden, cot, down, keep, send, grad_down, out_part):
    first_core = where[1] == 0
    shard = HD
    cols = d_gate_up.shape[1] // 3
    for chunk in range(tokens.shape[1] // 256):
        left = tokens[:, chunk * 256 : (chunk + 1) * 256]
        for third in range(3):
            here = pl.ds(third * cols, cols)
            terms = left_dot(left, d_gate_up[:, here]).reshape(2, 2, shard, cols)
            for pair in range(2):
                at = pl.ds((chunk * 2 + pair) * shard, shard)
                one, two = terms[pair, 0], terms[pair, 1]
                keep[at, here] = jnp.where(first_core, one, two).astype(BF16)
                send[at, here] = jnp.where(first_core, two, one).astype(BF16)
    for chunk in range(hidden.shape[1] // 384):
        here = pl.ds(chunk * 384, 384)
        grad_down[here, :] = left_dot(hidden[:, here], cot[...]).astype(BF16)
    for chunk in range(hidden.shape[0] // 128):
        at = pl.ds(chunk * 128, 128)
        out_part[at, :] = dot(hidden[at, :], down[...]).astype(BF16)


def pick_kernel(piece, side, gate, up, out):
    for j in range(SIDE):

        @pl.when(side[0] == j)
        def _():
            pieces = []
            for weight in (gate, up):
                values = weight[...].astype(F32)
                for begin in range(j * piece, values.shape[1], SIDE * piece):
                    pieces.append(values[:, begin : begin + piece])
            out[...] = jnp.concatenate(pieces, axis=1).astype(BF16)


def place_kernel(piece, shards_count, *refs):
    side = refs[0]
    big, down, small = (refs[1 + i * SIDE : 1 + (i + 1) * SIDE] for i in range(3))
    weights = refs[1 + 3 * SIDE : 6 + 3 * SIDE]
    outs = refs[6 + 3 * SIDE : -3]
    big_all, down_all, small_all = refs[-3:]
    for k in range(SIDE):
        big_all[side[0] ^ k] = big[k][...]
        down_all[side[0] ^ k] = down[k][...]
        small_all[side[0] ^ k] = small[k][...]
    out_query, out_key, out_value, out_out, out_gate, out_up, out_down, out_gains = outs
    ff_cols = piece * shards_count
    for j in range(SIDE):
        mine = small_all[j].astype(F32)
        begin = 0
        for out in (out_query, out_key, out_value, out_out):
            count = out.shape[1] // SIDE
            out[:, j * count : (j + 1) * count] = mine[:, begin : begin + count]
            begin += count
        out_gains[...] = mine[:, begin:] if j == 0 else out_gains[...] + mine[:, begin:]
        out_down[j * piece : (j + 1) * piece, :] = down_all[j].astype(F32)
    for which, out in enumerate((out_gate, out_up)):
        pieces = []
        both = [
            big_all[j, :, which * ff_cols : (which + 1) * ff_cols].astype(F32)
            for j in range(SIDE)
        ]
        for p in range(shards_count):
            for j in range(SIDE):
                pieces.append(both[j][:, p * piece : (p + 1) * piece])
        out[...] = jnp.concatenate(pieces, axis=1)

    def products(pairs):
        return sum(
            jnp.sum(out[...] * weight[...].astype(F32), axis=1, keepdims=True)
            for out, weight in pairs
        )

    attn = products(zip((out_query, out_key, out_value), weights[:3]))
    ffn = products(zip((out_gate, out_up), weights[3:]))
    lane = lanes(out_gains.shape)
    out_gains[...] = jnp.where(lane == 2, attn, jnp.where(lane == 3, ffn, out_gains[...]))


def shards(
    inputs,
    doc_ids,
    w_query,
    w_key,
    w_value,
    w_out,
    w_gate,
    w_up,
    w_down,
    attn_gain,
    ffn_gain,
    query_gain,
    key_gain,
    cotangent,
):
    rows, width = inputs.shape[1:]
    seqs = lax.axis_size("seq")
    dps = lax.axis_size("dp")
    me = lax.axis_index("seq")
    side = me % SIDE
    length = rows * seqs
    half = rows * SIDE
    shard = w_query.shape[0]
    q_cols = H * HD // SIDE
    kv_cols = KV * HD // SIDE
    ff = w_gate.shape[1]
    ff_cols = ff // SIDE
    piece = w_down.shape[0] // SIDE
    tall = max(piece, shard)
    cols = q_cols + 2 * kv_cols

    def columns(weight, count):
        return lax.dynamic_slice_in_dim(weight, side * count, count, axis=1)

    def out(*shape, dtype=F32):
        return jax.ShapeDtypeStruct(shape, dtype)

    params = pltpu.CompilerParams(vmem_limit_bytes=VMEM_LIMIT)

    tokens = inputs[0]
    cot = cotangent[0]
    mine = lax.axis_index("dp")
    few = HD // dps
    smem = pl.BlockSpec(memory_space=pltpu.SMEM)
    me_ref = me.astype(jnp.int32).reshape(1)
    attn_pack = pl.pallas_call(
        functools.partial(pack_kernel, few),
        out_shape=out(shard + 16, cols + width, dtype=BF16),
        in_specs=[smem] + [pl.BlockSpec(memory_space=pl.ANY)] * 4 + whole(1),
        out_specs=pl.BlockSpec(memory_space=pl.ANY),
        scratch_shapes=[pltpu.VMEM((16, cols + width), BF16), pltpu.SemaphoreType.DMA((5,))],
        compiler_params=params,
    )(
        jnp.stack([side, mine]).astype(jnp.int32),
        w_query,
        w_key,
        w_value,
        w_out,
        jnp.concatenate([attn_gain, ffn_gain, query_gain, key_gain])[None],
    )
    attn_all = lax.all_gather(attn_pack, "dp", axis=0, tiled=False)
    ids = jnp.pad(doc_ids.astype(BF16), ((0, 15), (0, width - rows)))
    message = jnp.concatenate([tokens, ids], axis=0)
    token_parts = [message] + [swap(message, "seq", k) for k in range(1, SIDE)]
    earlier = lax.ppermute(message, "seq", [(i, i ^ SIDE) for i in range(SIDE)])
    token_parts.append(earlier)
    for k in range(1, SIDE):
        token_parts.append(lax.ppermute(earlier, "seq", [(i, i ^ k) for i in range(SIDE, seqs)]))
    cot_parts = gather_side(cot)

    side_ref = side.astype(jnp.int32).reshape(1)
    picked = pl.pallas_call(
        functools.partial(pick_kernel, piece),
        out_shape=out(shard, 2 * ff_cols, dtype=BF16),
        in_specs=[smem] + whole(2),
        out_specs=whole(1)[0],
        compiler_params=params,
    )(side_ref, w_gate, w_up)
    down_piece = lax.dynamic_slice_in_dim(w_down, side * piece, piece, axis=0)
    pack = jnp.concatenate(
        [
            jnp.pad(picked, ((0, tall - shard), (0, 0))),
            jnp.pad(down_piece, ((0, tall - piece), (0, 0))),
        ],
        axis=1,
    )
    packed = lax.all_gather(pack, "dp", axis=0, tiled=False)
    w_qkv = attn_all[:, :shard, :cols].reshape(width, cols)
    wo = attn_all[:, :shard, cols:].reshape(H * HD, width)
    w_gate_up = packed[:, :shard, : 2 * ff_cols].reshape(width, 2 * ff_cols)
    wd = packed[:, :piece, 2 * ff_cols :].reshape(ff_cols, width)

    freqs = BASE ** (-(jnp.arange(HD // 2, dtype=F32) * (2.0 / HD)))
    freqs = jnp.concatenate([freqs] * 4)
    angles = jnp.arange(length, dtype=jnp.int32).astype(F32)[:, None] * freqs[None, :]

    normed, q_raw, k_raw, query, key, value, mixed, gains, cosine, sine, bounds = pl.pallas_call(
        functools.partial(forward_kernel, seqs),
        out_shape=(
            out(length, width, dtype=BF16),
            out(half, q_cols),
            out(length, kv_cols),
            out(half, q_cols, dtype=BF16),
            out(length, kv_cols, dtype=BF16),
            out(length, kv_cols, dtype=BF16),
            out(half, q_cols, dtype=BF16),
            out(16, width),
            out(length, 128),
            out(length, 128),
            out(8, 128),
        ),
        in_specs=[smem] + whole(seqs + 3),
        out_specs=tuple(whole(11)),
        scratch_shapes=[pltpu.VMEM((length, 128), BF16)] * 2,
        compiler_params=params,
        cost_estimate=pl.CostEstimate(
            flops=10_000_000_000, bytes_accessed=10_000_000, transcendentals=2_000_000
        ),
    )(me_ref, *token_parts, attn_all, jnp.cos(angles), jnp.sin(angles))
    attn_g = gains[0:1]
    ffn_g = gains[1:2]

    mixed = tie(mixed, *cot_parts)
    mixed_parts = scatter_side([mixed[k * rows : (k + 1) * rows] for k in range(SIDE)])
    attended_parts = jnp.stack(mixed_parts)
    attended = jnp.concatenate(
        [
            lax.dynamic_index_in_dim(attended_parts, side ^ j, axis=0, keepdims=False)
            for j in range(SIDE)
        ],
        axis=1,
    )
    states = tokens.astype(F32)
    resid = states + dot(attended, wo)
    normal2, inverse2 = norm_parts(resid)
    normed2 = (normal2 * ffn_g).astype(BF16)

    normed2_all = jnp.concatenate(gather_side(normed2), axis=0)
    attended_parts = gather_side(tie(attended, normed2_all))
    cot_all = jnp.concatenate(cot_parts, axis=0)
    gate_up = dot(normed2_all, w_gate_up)
    gate, upper = gate_up[:, :ff_cols], gate_up[:, ff_cols:]
    d_hidden = right_dot(cot_all, wd)
    sigmoid_gate = jax.nn.sigmoid(gate)
    active = gate * sigmoid_gate
    hidden = (active * upper).astype(BF16)
    d_gate = d_hidden * upper * sigmoid_gate * (1.0 + gate * (1.0 - sigmoid_gate))
    d_upper = d_hidden * active
    d_gate_up = jnp.concatenate([d_gate.astype(BF16), d_upper.astype(BF16)], axis=1)
    d_normed2_part = right_dot(d_gate_up, w_gate_up).astype(BF16)

    def scatter_rows(blocks):
        return scatter_side([blocks[k * rows : (k + 1) * rows] for k in range(SIDE)])

    def sum_parts(received):
        return sum(part.astype(F32) for part in received)

    d_normed2_parts = scatter_rows(d_normed2_part)

    core = mine % 2
    where = jnp.stack([me, core]).astype(jnp.int32)
    gate_up_keep, gate_up_send, grad_down, down_part = pl.pallas_call(
        terms_kernel,
        out_shape=(
            out(width // 2, 2 * ff_cols, dtype=BF16),
            out(width // 2, 2 * ff_cols, dtype=BF16),
            out(ff_cols, width, dtype=BF16),
            out(half, width, dtype=BF16),
        ),
        in_specs=[smem] + whole(5),
        out_specs=tuple(whole(4)),
        compiler_params=params,
        cost_estimate=pl.CostEstimate(
            flops=10_000_000_000, bytes_accessed=20_000_000, transcendentals=0
        ),
    )(where, normed2_all, tie(d_gate_up, d_normed2_part), hidden, cot_all, wd)
    down_share = lax.psum_scatter(grad_down, "dp", scatter_dimension=0, tiled=True)
    gate_up_got = swap(gate_up_send, "dp", 1)
    d_normed2_parts[0] = tie(d_normed2_parts[0], down_part)
    d_normed2 = sum_parts(d_normed2_parts)

    d_resid = cot.astype(F32) + norm_back(d_normed2 * ffn_g, normal2, inverse2)
    d_resid_low = d_resid.astype(BF16)
    d_attended = right_dot(d_resid_low, wo).astype(BF16)
    out_cols = width // SIDE
    d_messages = scatter_side(
        [
            jnp.concatenate(
                [
                    lax.dynamic_slice_in_dim(d_attended, (side ^ k) * q_cols, q_cols, axis=1),
                    lax.dynamic_slice_in_dim(d_resid_low, (side ^ k) * out_cols, out_cols, axis=1),
                ],
                axis=1,
            )
            for k in range(SIDE)
        ]
    )
    gate_up_sum = added(gate_up_keep, tie(gate_up_got, d_attended))
    gate_up_parts = send_along_z(gate_up_sum.reshape(4, 2, shard, -1), mine)
    down_parts = scatter_rows(tie(down_part, *d_messages))

    d_q_raw, d_kv_raw, attn_keep, attn_send = pl.pallas_call(
        backward_kernel,
        out_shape=(
            out(half, q_cols, dtype=BF16),
            out(length, 2 * kv_cols, dtype=BF16),
            out(width // 2, cols + out_cols + 128, dtype=BF16),
            out(width // 2, cols + out_cols + 128, dtype=BF16),
        ),
        in_specs=[smem] + whole(2 * SIDE + 10),
        out_specs=tuple(whole(4)),
        scratch_shapes=[
            pltpu.VMEM((length, 128), BF16),
            pltpu.VMEM((length, 128), BF16),
            pltpu.VMEM((2, length, 128), F32),
            pltpu.VMEM((2, length, 128), F32),
            pltpu.VMEM((half, q_cols), F32),
            pltpu.VMEM((half, q_cols), BF16),
            pltpu.VMEM((length, 128), F32),
            pltpu.VMEM((half, width), BF16),
            pltpu.VMEM((half, out_cols), BF16),
        ],
        compiler_params=params,
        cost_estimate=pl.CostEstimate(
            flops=14_000_000_000, bytes_accessed=10_000_000, transcendentals=2_000_000
        ),
    )(
        where,
        *d_messages,
        *attended_parts,
        query,
        key,
        value,
        q_raw,
        k_raw,
        cosine,
        sine,
        normed,
        gains,
        bounds,
    )
    x = mine // 2 % 2
    z = mine // 4
    gate_up_parts[0] = tie(gate_up_parts[0], d_kv_raw)
    gate_up_sum = added(*gate_up_parts)
    gate_up_got = swap(take(gate_up_sum, 1 - x, 0), "dp", 2)
    attn_got = swap(attn_send, "dp", 1)
    from_later = lax.ppermute(
        d_kv_raw[half:], "seq", [(i, i - SIDE) for i in range(SIDE, seqs)]
    )
    attn_sum = added(attn_keep, tie(attn_got, gate_up_sum)).reshape(4, 2, shard, -1)
    attn_parts = send_along_z(attn_sum, mine)
    gate_up_share = added(take(gate_up_sum, x, 0), tie(gate_up_got, attn_sum))
    gate_up_other = swap(gate_up_share, "seq", SIDE)
    d_kv = added(d_kv_raw[:half], tie(from_later, gate_up_share))
    d_qkv = jnp.concatenate([d_q_raw, d_kv], axis=1)
    d_normed_part = right_dot(d_qkv, w_qkv).astype(BF16)
    d_normed_parts = scatter_rows(d_normed_part)
    attn_parts[0] = tie(attn_parts[0], d_normed_part)
    attn_sum = added(*attn_parts)
    attn_got = swap(take(attn_sum, 1 - x, 0), "dp", 2)
    gate_up_share = added(gate_up_share, tie(gate_up_other, attn_sum))
    gate_up_parts = gather_side(gate_up_share)
    attn_share = added(take(attn_sum, x, 0), tie(attn_got, gate_up_share))
    attn_other = swap(attn_share, "seq", SIDE)
    down_other = swap(down_share, "seq", SIDE)
    down_parts[0] = tie(down_parts[0], attn_share)
    block_out = (resid + sum_parts(down_parts)).astype(BF16)
    d_normed_parts[0] = tie(d_normed_parts[0], attn_share)
    d_normed = sum_parts(d_normed_parts)
    attn_share = added(attn_share, tie(attn_other, d_normed))
    attn_parts = gather_side(attn_share)
    down_share = added(down_share, tie(down_other, attn_share))
    down_parts = gather_side(down_share)
    normal1, inverse1 = norm_parts(states)
    grad_inputs = d_resid + norm_back(d_normed * attn_g, normal1, inverse1)

    outs = pl.pallas_call(
        functools.partial(place_kernel, piece, dps),
        out_shape=(
            out(shard, H * HD),
            out(shard, KV * HD),
            out(shard, KV * HD),
            out(shard, width),
            out(shard, ff),
            out(shard, ff),
            out(SIDE * piece, width),
            out(shard, 128),
        ),
        in_specs=[smem] + whole(3 * SIDE + 5),
        out_specs=tuple(whole(8)),
        scratch_shapes=[
            pltpu.VMEM((SIDE,) + gate_up_share.shape, BF16),
            pltpu.VMEM((SIDE,) + down_share.shape, BF16),
            pltpu.VMEM((SIDE,) + attn_share.shape, BF16),
        ],
        compiler_params=params,
    )(
        side_ref,
        *gate_up_parts,
        *down_parts,
        *attn_parts,
        w_query,
        w_key,
        w_value,
        w_gate,
        w_up,
    )
    out_query, out_key, out_value, out_out, out_gate, out_up, out_down, out_gains = outs
    return (
        block_out[None],
        grad_inputs[None],
        out_query,
        out_key,
        out_value,
        out_out,
        out_gate,
        out_up,
        out_down,
        out_gains[:, 2] / attn_gain.astype(F32),
        out_gains[:, 3] / ffn_gain.astype(F32),
        out_gains[:few, 0],
        out_gains[:few, 1],
    )


def solution(mesh):
    tokens = P("dp", "seq", None)
    weight = P("dp", None)
    gain = P("dp")
    return jax.shard_map(
        shards,
        mesh=mesh,
        in_specs=(tokens, P("dp", "seq")) + (weight,) * 7 + (gain,) * 4 + (tokens,),
        out_specs=(tokens, tokens) + (weight,) * 7 + (gain,) * 4,
        check_vma=False,
    )
```

```python
import functools

import jax
import jax.numpy as jnp
from jax import lax
from jax.experimental import pallas as pl
from jax.experimental.pallas import tpu as pltpu
from jax.sharding import PartitionSpec as P

H = 16
KV = 8
HD = 64
SIDE = 4

EPS = 1e-05
BASE = 1000000.0
MASKED = -1e30
SCALE = HD ** (-0.5)
BF16 = jnp.bfloat16
F32 = jnp.float32
VMEM_LIMIT = 50 * 1024 * 1024


def left_dot(left, right):
    return lax.dot_general(left, right, (((0,), (0,)), ((), ())), preferred_element_type=F32)


def right_dot(left, right):
    return lax.dot_general(left, right, (((1,), (1,)), ((), ())), preferred_element_type=F32)


def dot(left, right):
    return lax.dot_general(left, right, (((1,), (0,)), ((), ())), preferred_element_type=F32)


def norm_parts(values):
    inverse = lax.rsqrt(jnp.mean(values * values, axis=-1, keepdims=True) + EPS)
    return (values * inverse, inverse)


def norm_back(incoming, normal, inverse):
    return inverse * (incoming - normal * jnp.mean(incoming * normal, axis=-1, keepdims=True))


def swap(block, axis, step):
    size = lax.axis_size(axis)
    return lax.ppermute(block, axis, [(i, i ^ step) for i in range(size)])


def gather_side(block):
    return [block] + [swap(block, "seq", k) for k in range(1, SIDE)]


def scatter_side(blocks):
    return [blocks[0]] + [swap(blocks[k], "seq", k) for k in range(1, SIDE)]


def tie(value, *after):
    return lax.optimization_barrier((value,) + after)[0]


def take(array, index, axis):
    return lax.dynamic_index_in_dim(array, index, axis=axis, keepdims=False)


def added(*pieces):
    return sum(piece.astype(F32) for piece in pieces).astype(BF16)


def send_along_z(total, mine):
    z = mine >> 2
    return [take(total, z, 0)] + [swap(take(total, z ^ k, 0), "dp", 4 * k) for k in range(1, 4)]


def whole(count):
    return [pl.BlockSpec(memory_space=pltpu.VMEM)] * count


def lanes(shape):
    return lax.broadcasted_iota(jnp.int32, shape, len(shape) - 1)


def head_mean(values):
    row = lax.broadcasted_iota(jnp.int32, (128, 128), 0)
    ones = jnp.where(row // HD == lanes((128, 128)) // HD, 1.0 / HD, 0.0).astype(BF16)
    high = values.astype(BF16)
    rest = (values - high.astype(F32)).astype(BF16)
    return dot(high, ones) + dot(rest, ones)


def partner(values):
    return jnp.where(
        lanes(values.shape) % HD < HD // 2,
        pltpu.roll(values, 128 - HD // 2, 1),
        pltpu.roll(values, HD // 2, 1),
    )


def doubled(pair, head):
    other = pltpu.roll(pair.astype(F32), HD, 1).astype(pair.dtype)
    first = lanes(pair.shape) < HD
    return jnp.where(first, pair, other) if head == 0 else jnp.where(first, other, pair)


def two_heads(block):
    first = lanes(block.shape) < HD
    zero = jnp.zeros_like(block)
    return jnp.concatenate([jnp.where(first, block, zero), jnp.where(first, zero, block)], axis=0)


def sublanes(shape):
    return lax.broadcasted_iota(jnp.int32, shape, len(shape) - 2)


def pack_kernel(few, where, query, key, value, out_weight, gains, pack, scratch, sems):
    side, mine = where[0], where[1]
    shard, width = out_weight.shape
    copies = []
    begin = 0
    for weight in (query, key, value):
        count = weight.shape[1] // SIDE
        at = pl.ds(pl.multiple_of(side * count, count), count)
        copies.append((weight.at[:, at], pack.at[pl.ds(0, shard), pl.ds(begin, count)]))
        begin += count
    copies.append((out_weight, pack.at[pl.ds(0, shard), pl.ds(begin, width)]))
    copies = [
        pltpu.make_async_copy(source, target, sems.at[index])
        for index, (source, target) in enumerate(copies)
    ]
    for copy in copies:
        copy.start()

    def spread(gain, count, lane_count):
        row = jnp.concatenate([gain] * (lane_count // count), axis=1)
        return row, lanes(row.shape)

    all_gains = gains[...].astype(F32)
    rows = []
    for gain in (all_gains[:, :shard], all_gains[:, shard : 2 * shard]):
        row, lane = spread(gain, shard, width)
        rows.append(jnp.where(lane // shard == mine, row, 0.0))
    for index in range(2):
        gain = all_gains[:, 2 * shard + index * few : 2 * shard + (index + 1) * few]
        row, lane = spread(gain, few, 128)
        row = jnp.where(lane % HD // few == mine, row, 0.0)
        rows.append(jnp.concatenate([row, jnp.zeros((1, width - 128), F32)], axis=1))
    at = sublanes((16, width))
    extra = jnp.zeros((16, width), F32)
    for index, row in enumerate(rows):
        extra = jnp.where(at == index, row, extra)
    extra = jnp.concatenate([extra, jnp.zeros((16, begin), F32)], axis=1)
    scratch[...] = extra.astype(BF16)
    last = pltpu.make_async_copy(scratch, pack.at[pl.ds(shard, 16), :], sems.at[len(copies)])
    last.start()
    for copy in copies + [last]:
        copy.wait()


def start_of(place, cuts):
    return jnp.where(place >= cuts[1], cuts[1], jnp.where(place >= cuts[0], cuts[0], 0.0))


def forward_kernel(parts, me, *refs):
    token_refs = refs[:parts]
    packed, cos_table, sin_table = refs[parts : parts + 3]
    normed_out, q_raw, k_raw, query, key, value, mixed, gains = refs[parts + 3 : parts + 11]
    cosine, sine, bounds, k_two, v_two = refs[parts + 11 :]
    rows = query.shape[0] // SIDE
    width = token_refs[0].shape[1]
    q_cols = query.shape[1]
    cols = q_cols + 2 * key.shape[1]
    shard = packed.shape[1] - 16
    weight = packed[:, :shard, :cols].reshape(width, cols)
    gains[...] = jnp.sum(packed[:, shard:, :width].astype(F32), axis=0)
    gain, q_gain, k_gain = gains[0:1, :], gains[2:3, :128], gains[3:4, :128]

    bases = [(me[0] ^ part) * rows for part in range(parts)]
    row_places = [(lanes((1, rows)) + base).astype(F32) for base in bases]
    cuts = []
    for number in (1.0, 2.0):
        least = jnp.full((1, rows), 4096.0, F32)
        for part in range(parts):
            ids = token_refs[part][rows:, :rows].astype(F32)[0:1]
            least = jnp.minimum(least, jnp.where(ids == number, row_places[part], 4096.0))
        cuts.append(jnp.min(least, axis=1, keepdims=True))
    for index in range(2):
        bounds[index : index + 1, :] = jnp.broadcast_to(cuts[index], (1, 128))
    at_cut = []
    all_places = sublanes(cos_table.shape).astype(F32)
    for cut in cuts:
        there = all_places == cut
        at_cut.append(
            [
                jnp.sum(jnp.where(there, table[...], 0.0), axis=0, keepdims=True)
                for table in (cos_table, sin_table)
            ]
        )
    sign = jnp.where(lanes((1, 128)) % HD < HD // 2, -1.0, 1.0)

    for part in range(parts):
        at = pl.ds(part * rows, rows)
        states = token_refs[part][:rows, :].astype(F32)
        inverse = lax.rsqrt(jnp.mean(states * states, axis=-1, keepdims=True) + EPS)
        normed = (states * inverse * gain).astype(BF16)
        there = pl.ds(pl.multiple_of(bases[part], rows), rows)
        place = (sublanes((rows, 128)) + bases[part]).astype(F32)
        cos_cut = jnp.where(
            place >= cuts[1], at_cut[1][0], jnp.where(place >= cuts[0], at_cut[0][0], 1.0)
        )
        sin_cut = jnp.where(
            place >= cuts[1], at_cut[1][1], jnp.where(place >= cuts[0], at_cut[0][1], 0.0)
        )
        cos = cos_table[there, :] * cos_cut + sin_table[there, :] * sin_cut
        sin = (sin_table[there, :] * cos_cut - cos_table[there, :] * sin_cut) * sign
        cosine[at, :] = cos
        sine[at, :] = sin
        normed_out[at, :] = normed
        if part < SIDE:
            raw = dot(normed, weight)
            raw_q, raw_kv = raw[:, :q_cols], raw[:, q_cols:]
            q_raw[at, :] = raw_q
            for pair in range(q_cols // 128):
                here = pl.ds(pair * 128, 128)
                one = raw_q[:, pair * 128 : (pair + 1) * 128]
                scaled = one * lax.rsqrt(head_mean(one * one) + EPS) * q_gain
                query[at, here] = (scaled * cos + partner(scaled) * sin).astype(BF16)
        else:
            raw_kv = dot(normed, weight[:, q_cols:])
        one = raw_kv[:, :128]
        k_raw[at, :] = one
        scaled = one * lax.rsqrt(head_mean(one * one) + EPS) * k_gain
        key[at, :] = (scaled * cos + partner(scaled) * sin).astype(BF16)
        value[at, :] = raw_kv[:, 128:].astype(BF16)
    k_place = jnp.concatenate(row_places, axis=1)
    for pair in range(q_cols // 128):
        here = pl.ds(pair * 128, 128)
        k_two[...] = doubled(key[...], pair)
        v_two[...] = doubled(value[...], pair)

        @pl.loop(0, SIDE)
        def _(step):
            at = pl.ds(pl.multiple_of(step * rows, rows), rows)
            q_place = (sublanes((rows, 1)) + (me[0] ^ step) * rows).astype(F32)
            q_place = jnp.concatenate([q_place, q_place], axis=0)
            allowed = (k_place <= q_place) & (k_place >= start_of(q_place, cuts))
            scores = right_dot(two_heads(query[at, here]), k_two[...]) * SCALE
            scores = jnp.where(allowed, scores, MASKED)
            expd = jnp.exp(scores - jnp.max(scores, axis=-1, keepdims=True))
            probs = (expd * (1.0 / jnp.sum(expd, axis=-1, keepdims=True))).astype(BF16)
            both = dot(probs, v_two[...])
            mixed[at, here] = jnp.where(
                lanes((rows, 128)) < HD, both[:rows], both[rows:]
            ).astype(BF16)


def backward_kernel(me, *refs):
    d_mixed, attended = refs[:SIDE], refs[SIDE : 2 * SIDE]
    query, key, value, q_raw, k_raw, cosine, sine, normed = refs[2 * SIDE : 2 * SIDE + 8]
    gains, bounds, d_q_raw, d_kv_raw, keep, send = refs[2 * SIDE + 8 : 2 * SIDE + 14]
    k_two, v_two, d_k, d_v, d_q, d_both, k_place, all_attended, d_cols = refs[2 * SIDE + 14 :]
    rows = d_mixed[0].shape[0]
    length = key.shape[0]
    q_cols = query.shape[1]
    pairs = q_cols // 128
    q_gain, k_gain = gains[2:3, :128], gains[3:4, :128]
    cuts = [bounds[0:1, :], bounds[1:2, :]]
    for part in range(SIDE):
        at = pl.ds(part * rows, rows)
        d_both[at, :] = d_mixed[part][:, :q_cols]
        d_cols[at, :] = d_mixed[part][:, q_cols:]
        all_attended[at, :] = attended[part][...]
    for part in range(length // rows):
        base = (me[0] ^ part) * rows
        k_place[pl.ds(part * rows, rows), :] = (sublanes((rows, 128)) + base).astype(F32)
    for pair in range(pairs):
        here = pl.ds(pair * 128, 128)
        k_two[...] = doubled(key[...], pair)
        v_two[...] = doubled(value[...], pair)
        d_k[pair] = jnp.zeros((length, 128), F32)
        d_v[pair] = jnp.zeros((length, 128), F32)

        @pl.loop(0, SIDE)
        def _(step):
            at = pl.ds(pl.multiple_of(step * rows, rows), rows)
            q_place = (lanes((1, rows)) + (me[0] ^ step) * rows).astype(F32)
            allowed = (k_place[...] <= q_place) & (k_place[...] >= start_of(q_place, cuts))
            allowed = jnp.concatenate([allowed, allowed], axis=1)
            q_two = two_heads(query[at, here])
            d_two = two_heads(d_both[at, here])
            scores = jnp.where(allowed, right_dot(k_two[...], q_two) * SCALE, MASKED)
            expd = jnp.exp(scores - jnp.max(scores, axis=0, keepdims=True))
            probs = expd * (1.0 / jnp.sum(expd, axis=0, keepdims=True))
            d_probs = right_dot(v_two[...], d_two)
            delta = jnp.sum(probs * d_probs, axis=0, keepdims=True)
            d_scores = (probs * (d_probs - delta)).astype(BF16)
            d_v[pair] += dot(probs.astype(BF16), d_two)
            d_k[pair] += dot(d_scores, q_two)
            both = left_dot(d_scores, k_two[...])
            d_q[at, here] = jnp.where(lanes((rows, 128)) < HD, both[:rows], both[rows:]) * SCALE

    first = lanes((rows, 128)) < HD
    sums = [jnp.zeros((1, 128), F32), jnp.zeros((1, 128), F32)]

    def back(incoming, raw, gain, at, which):
        inverse = lax.rsqrt(head_mean(raw * raw) + EPS)
        normal = raw * inverse
        incoming = incoming.astype(BF16).astype(F32)
        turned = incoming * cosine[at, :] - partner(incoming) * sine[at, :]
        sums[which] = sums[which] + jnp.sum(turned * normal, axis=0, keepdims=True)
        turned = turned * gain
        return (inverse * (turned - normal * head_mean(turned * normal))).astype(BF16)

    def joined(pieces):
        pieces = [piece + pltpu.roll(piece, HD, 1) for piece in pieces]
        return jnp.where(first, pieces[0], pieces[1])

    for part in range(length // rows):
        at = pl.ds(part * rows, rows)
        if part < SIDE:
            for pair in range(pairs):
                here = pl.ds(pair * 128, 128)
                d_q_raw[at, here] = back(d_q[at, here], q_raw[at, here], q_gain, at, 0)
        d_key = joined([d_k[pair, at, :] for pair in range(pairs)]) * SCALE
        d_kv_raw[at, :128] = back(d_key, k_raw[at, :], k_gain, at, 1)
        d_kv_raw[at, 128:] = joined([d_v[pair, at, :] for pair in range(pairs)]).astype(BF16)

    half = SIDE * rows
    width = normed.shape[1]
    shard = HD
    few = HD * shard // width
    sums = [total + pltpu.roll(total, HD, 1) for total in sums]
    row, lane = sublanes((8, 128)), lanes((8, 128))

    def gain_block(p):
        there = (row < few) & (lane == p * few + row)
        sides = [jnp.sum(jnp.where(there, total, 0.0), axis=1, keepdims=True) for total in sums]
        block = jnp.where(lane == 0, sides[0], jnp.where(lane == 1, sides[1], 0.0))
        return jnp.concatenate([block, jnp.zeros((shard - 8, 128), F32)], axis=0)

    first_core = me[1] == 0
    for chunk in range(width // 256):
        here = pl.ds(chunk * 256, 256)
        terms = jnp.concatenate(
            [
                left_dot(normed[:half, here], d_q_raw[...]),
                left_dot(normed[:, here], d_kv_raw[...]),
                left_dot(all_attended[:, here], d_cols[...]),
            ],
            axis=1,
        )
        for pair in range(256 // (2 * shard)):
            blocks = []
            for core in range(2):
                begin = (2 * pair + core) * shard
                p = begin // shard + chunk * (256 // shard)
                blocks.append(
                    jnp.concatenate([terms[begin : begin + shard], gain_block(p)], axis=1)
                )
            at = pl.ds((chunk * (256 // shard) // 2 + pair) * shard, shard)
            keep[at, :] = jnp.where(first_core, blocks[0], blocks[1]).astype(BF16)
            send[at, :] = jnp.where(first_core, blocks[1], blocks[0]).astype(BF16)


def terms_kernel(where, tokens, d_gate, d_up, hidden, cot, down, keep, send, out_part, grad_down):
    first_core = where[1] == 0
    shard = HD
    cols = d_gate.shape[1]
    tall = keep.shape[0] // 8
    width = tokens.shape[1]
    piece = hidden.shape[1] // 16
    wide = 2 * cols - 2 * width

    def store(block, begin, here, one, two):
        at = pl.ds(block * tall + begin, one.shape[0])
        keep[at, here] = jnp.where(first_core, one, two).astype(BF16)
        send[at, here] = jnp.where(first_core, two, one).astype(BF16)

    for chunk in range(width // 256):
        left = tokens[:, chunk * 256 : (chunk + 1) * 256]
        for which, right in enumerate((d_gate, d_up)):
            here = pl.ds(which * cols, cols)
            terms = left_dot(left, right[...]).reshape(2, 2, shard, cols)
            for pair in range(2):
                store(chunk * 2 + pair, 0, here, terms[pair, 0], terms[pair, 1])
    for chunk in range(hidden.shape[1] // 384):
        here = pl.ds(chunk * 384, 384)
        grad_down[here, :] = left_dot(hidden[:, here], cot[...])

    def folded(p):
        rows = grad_down[p * piece : (p + 1) * piece, :]
        rest = [rows[64:, j * wide : (j + 1) * wide] for j in range(width // wide)]
        return jnp.concatenate([rows[:32], rows[32:64], jnp.concatenate(rest, axis=0)], axis=1)

    for block in range(8):
        store(block, shard, pl.ds(0, 2 * cols), folded(2 * block), folded(2 * block + 1))
    for chunk in range(hidden.shape[0] // 128):
        at = pl.ds(chunk * 128, 128)
        out_part[at, :] = dot(hidden[at, :], down[...]).astype(BF16)


def pick_kernel(piece, side, gate, up, out):
    for j in range(SIDE):

        @pl.when(side[0] == j)
        def _():
            pieces = []
            for weight in (gate, up):
                values = weight[...].astype(F32)
                for begin in range(j * piece, values.shape[1], SIDE * piece):
                    pieces.append(values[:, begin : begin + piece])
            out[...] = jnp.concatenate(pieces, axis=1).astype(BF16)


def place_kernel(piece, shards_count, *refs):
    side = refs[0]
    big, small = refs[1 : 1 + SIDE], refs[1 + SIDE : 1 + 2 * SIDE]
    weights = refs[1 + 2 * SIDE : 6 + 2 * SIDE]
    outs = refs[6 + 2 * SIDE : -2]
    big_all, small_all = refs[-2:]
    for k in range(SIDE):
        big_all[side[0] ^ k] = big[k][...]
        small_all[side[0] ^ k] = small[k][...]
    out_query, out_key, out_value, out_out, out_gate, out_up, out_down, out_gains = outs
    shard = out_gate.shape[0]
    ff_cols = piece * shards_count
    for j in range(SIDE):
        mine = small_all[j].astype(F32)
        begin = 0
        for out in (out_query, out_key, out_value, out_out):
            count = out.shape[1] // SIDE
            out[:, j * count : (j + 1) * count] = mine[:, begin : begin + count]
            begin += count
        out_gains[...] = mine[:, begin:] if j == 0 else out_gains[...] + mine[:, begin:]
        folded = big_all[j, shard:, :].astype(F32)
        width = out_down.shape[1]
        out_down[j * piece : j * piece + 32, :] = folded[:, :width]
        out_down[j * piece + 32 : j * piece + 64, :] = folded[:, width : 2 * width]
        rest = [folded[8 * i : 8 * i + 8, 2 * width :] for i in range(4)]
        out_down[j * piece + 64 : (j + 1) * piece, :] = jnp.concatenate(rest, axis=1)
    for which, out in enumerate((out_gate, out_up)):
        pieces = []
        both = [
            big_all[j, :shard, which * ff_cols : (which + 1) * ff_cols].astype(F32)
            for j in range(SIDE)
        ]
        for p in range(shards_count):
            for j in range(SIDE):
                pieces.append(both[j][:, p * piece : (p + 1) * piece])
        out[...] = jnp.concatenate(pieces, axis=1)

    def products(pairs):
        return sum(
            jnp.sum(out[...] * weight[...].astype(F32), axis=1, keepdims=True)
            for out, weight in pairs
        )

    attn = products(zip((out_query, out_key, out_value), weights[:3]))
    ffn = products(zip((out_gate, out_up), weights[3:]))
    lane = lanes(out_gains.shape)
    out_gains[...] = jnp.where(lane == 2, attn, jnp.where(lane == 3, ffn, out_gains[...]))


def shards(
    inputs,
    doc_ids,
    w_query,
    w_key,
    w_value,
    w_out,
    w_gate,
    w_up,
    w_down,
    attn_gain,
    ffn_gain,
    query_gain,
    key_gain,
    cotangent,
):
    rows, width = inputs.shape[1:]
    seqs = lax.axis_size("seq")
    dps = lax.axis_size("dp")
    me = lax.axis_index("seq").astype(jnp.uint32)
    side = me & (SIDE - 1)
    length = rows * seqs
    half = rows * SIDE
    shard = w_query.shape[0]
    q_cols = H * HD // SIDE
    kv_cols = KV * HD // SIDE
    ff = w_gate.shape[1]
    ff_cols = ff // SIDE
    piece = w_down.shape[0] // SIDE
    tall = max(piece, shard)
    cols = q_cols + 2 * kv_cols

    def columns(weight, count):
        return lax.dynamic_slice_in_dim(weight, side * count, count, axis=1)

    def out(*shape, dtype=F32):
        return jax.ShapeDtypeStruct(shape, dtype)

    params = pltpu.CompilerParams(vmem_limit_bytes=VMEM_LIMIT)

    tokens = inputs[0]
    cot = cotangent[0]
    mine = lax.axis_index("dp").astype(jnp.uint32)
    core, x, z = mine & 1, (mine >> 1) & 1, mine >> 2
    few = HD // dps
    smem = pl.BlockSpec(memory_space=pltpu.SMEM)
    me_ref = me.astype(jnp.int32).reshape(1)
    attn_pack = pl.pallas_call(
        functools.partial(pack_kernel, few),
        out_shape=out(shard + 16, cols + width, dtype=BF16),
        in_specs=[smem] + [pl.BlockSpec(memory_space=pl.ANY)] * 4 + whole(1),
        out_specs=pl.BlockSpec(memory_space=pl.ANY),
        scratch_shapes=[pltpu.VMEM((16, cols + width), BF16), pltpu.SemaphoreType.DMA((5,))],
        compiler_params=params,
    )(
        jnp.stack([side, mine]).astype(jnp.int32),
        w_query,
        w_key,
        w_value,
        w_out,
        jnp.concatenate([attn_gain, ffn_gain, query_gain, key_gain])[None],
    )
    attn_all = lax.all_gather(attn_pack, "dp", axis=0, tiled=False)
    ids = jnp.pad(doc_ids.astype(BF16), ((0, 15), (0, width - rows)))
    message = jnp.concatenate([tokens, ids], axis=0)
    token_parts = [message] + [swap(message, "seq", k) for k in range(1, SIDE)]
    earlier = lax.ppermute(message, "seq", [(i, i ^ SIDE) for i in range(SIDE)])
    token_parts.append(earlier)
    for k in range(1, SIDE):
        token_parts.append(lax.ppermute(earlier, "seq", [(i, i ^ k) for i in range(SIDE, seqs)]))
    cot_parts = gather_side(cot)

    side_ref = side.astype(jnp.int32).reshape(1)
    picked = pl.pallas_call(
        functools.partial(pick_kernel, piece),
        out_shape=out(shard, 2 * ff_cols, dtype=BF16),
        in_specs=[smem] + whole(2),
        out_specs=whole(1)[0],
        compiler_params=params,
    )(side_ref, w_gate, w_up)
    down_piece = lax.dynamic_slice_in_dim(w_down, side * piece, piece, axis=0)
    pack = jnp.concatenate(
        [
            jnp.pad(picked, ((0, tall - shard), (0, 0))),
            jnp.pad(down_piece, ((0, tall - piece), (0, 0))),
        ],
        axis=1,
    )
    packed = lax.all_gather(pack, "dp", axis=0, tiled=False)
    w_qkv = attn_all[:, :shard, :cols].reshape(width, cols)
    wo = attn_all[:, :shard, cols:].reshape(H * HD, width)
    w_gate_up = packed[:, :shard, : 2 * ff_cols].reshape(width, 2 * ff_cols)
    wd = packed[:, :piece, 2 * ff_cols :].reshape(ff_cols, width)

    freqs = BASE ** (-(jnp.arange(HD // 2, dtype=F32) * (2.0 / HD)))
    freqs = jnp.concatenate([freqs] * 4)
    angles = jnp.arange(length, dtype=jnp.int32).astype(F32)[:, None] * freqs[None, :]

    normed, q_raw, k_raw, query, key, value, mixed, gains, cosine, sine, bounds = pl.pallas_call(
        functools.partial(forward_kernel, seqs),
        out_shape=(
            out(length, width, dtype=BF16),
            out(half, q_cols),
            out(length, kv_cols),
            out(half, q_cols, dtype=BF16),
            out(length, kv_cols, dtype=BF16),
            out(length, kv_cols, dtype=BF16),
            out(half, q_cols, dtype=BF16),
            out(16, width),
            out(length, 128),
            out(length, 128),
            out(8, 128),
        ),
        in_specs=[smem] + whole(seqs + 3),
        out_specs=tuple(whole(11)),
        scratch_shapes=[pltpu.VMEM((length, 128), BF16)] * 2,
        compiler_params=params,
        cost_estimate=pl.CostEstimate(
            flops=10_000_000_000, bytes_accessed=10_000_000, transcendentals=2_000_000
        ),
    )(me_ref, *token_parts, attn_all, jnp.cos(angles), jnp.sin(angles))
    attn_g = gains[0:1]
    ffn_g = gains[1:2]

    mixed = tie(mixed, *cot_parts)
    mixed_parts = scatter_side([mixed[k * rows : (k + 1) * rows] for k in range(SIDE)])
    attended_parts = jnp.stack(mixed_parts)
    attended = jnp.concatenate(
        [
            lax.dynamic_index_in_dim(attended_parts, side ^ j, axis=0, keepdims=False)
            for j in range(SIDE)
        ],
        axis=1,
    )
    states = tokens.astype(F32)
    resid = states + dot(attended, wo)
    normal2, inverse2 = norm_parts(resid)
    normed2 = (normal2 * ffn_g).astype(BF16)

    normed2_all = jnp.concatenate(gather_side(tie(normed2, w_qkv)), axis=0)
    attended_parts = gather_side(tie(attended, normed2_all))
    cot_all = jnp.concatenate(cot_parts, axis=0)
    gate_up = dot(normed2_all, w_gate_up)
    gate, upper = gate_up[:, :ff_cols], gate_up[:, ff_cols:]
    d_hidden = right_dot(cot_all, wd)
    sigmoid_gate = jax.nn.sigmoid(gate)
    active = gate * sigmoid_gate
    hidden = (active * upper).astype(BF16)
    d_gate = d_hidden * upper * sigmoid_gate * (1.0 + gate * (1.0 - sigmoid_gate))
    d_upper = d_hidden * active
    d_gate, d_upper = d_gate.astype(BF16), d_upper.astype(BF16)
    d_gate_up = jnp.concatenate([d_gate, d_upper], axis=1)
    d_normed2_part = right_dot(d_gate_up, w_gate_up).astype(BF16)

    def scatter_rows(blocks):
        return scatter_side([blocks[k * rows : (k + 1) * rows] for k in range(SIDE)])

    def sum_parts(received):
        return sum(part.astype(F32) for part in received)

    d_normed2_parts = scatter_rows(d_normed2_part)

    where = jnp.stack([me, core]).astype(jnp.int32)
    gate_up_keep, gate_up_send, down_part = pl.pallas_call(
        terms_kernel,
        out_shape=(
            out(dps // 2 * (shard + 32), 2 * ff_cols, dtype=BF16),
            out(dps // 2 * (shard + 32), 2 * ff_cols, dtype=BF16),
            out(half, width, dtype=BF16),
        ),
        in_specs=[smem] + whole(6),
        out_specs=tuple(whole(3)),
        scratch_shapes=[pltpu.VMEM((ff_cols, width), F32)],
        compiler_params=params,
        cost_estimate=pl.CostEstimate(
            flops=10_000_000_000, bytes_accessed=20_000_000, transcendentals=0
        ),
    )(
        where,
        normed2_all,
        tie(d_gate, d_normed2_part, *attended_parts),
        d_upper,
        hidden,
        cot_all,
        wd,
    )
    d_normed2_parts[0] = tie(d_normed2_parts[0], down_part)
    d_normed2 = sum_parts(d_normed2_parts)
    gate_up_got = swap(tie(gate_up_send, d_normed2), "dp", 1)

    d_resid = cot.astype(F32) + norm_back(d_normed2 * ffn_g, normal2, inverse2)
    d_resid_low = d_resid.astype(BF16)
    d_attended = right_dot(d_resid_low, wo).astype(BF16)
    out_cols = width // SIDE
    d_messages = scatter_side(
        [
            jnp.concatenate(
                [
                    lax.dynamic_slice_in_dim(d_attended, (side ^ k) * q_cols, q_cols, axis=1),
                    lax.dynamic_slice_in_dim(d_resid_low, (side ^ k) * out_cols, out_cols, axis=1),
                ],
                axis=1,
            )
            for k in range(SIDE)
        ]
    )
    gate_up_sum = added(gate_up_keep, tie(gate_up_got, d_attended))
    gate_up_parts = send_along_z(gate_up_sum.reshape(4, 2, shard + 32, -1), mine)
    down_parts = scatter_rows(tie(down_part, *d_messages))

    d_q_raw, d_kv_raw, attn_keep, attn_send = pl.pallas_call(
        backward_kernel,
        out_shape=(
            out(half, q_cols, dtype=BF16),
            out(length, 2 * kv_cols, dtype=BF16),
            out(width // 2, cols + out_cols + 128, dtype=BF16),
            out(width // 2, cols + out_cols + 128, dtype=BF16),
        ),
        in_specs=[smem] + whole(2 * SIDE + 10),
        out_specs=tuple(whole(4)),
        scratch_shapes=[
            pltpu.VMEM((length, 128), BF16),
            pltpu.VMEM((length, 128), BF16),
            pltpu.VMEM((2, length, 128), F32),
            pltpu.VMEM((2, length, 128), F32),
            pltpu.VMEM((half, q_cols), F32),
            pltpu.VMEM((half, q_cols), BF16),
            pltpu.VMEM((length, 128), F32),
            pltpu.VMEM((half, width), BF16),
            pltpu.VMEM((half, out_cols), BF16),
        ],
        compiler_params=params,
        cost_estimate=pl.CostEstimate(
            flops=14_000_000_000, bytes_accessed=10_000_000, transcendentals=2_000_000
        ),
    )(
        where,
        *d_messages,
        *attended_parts,
        query,
        key,
        value,
        q_raw,
        k_raw,
        cosine,
        sine,
        normed,
        gains,
        bounds,
    )
    gate_up_parts[0] = tie(gate_up_parts[0], d_kv_raw)
    gate_up_sum = added(*gate_up_parts)
    gate_up_got = swap(take(gate_up_sum, 1 - x, 0), "dp", 2)
    attn_got = swap(attn_send, "dp", 1)
    from_later = lax.ppermute(
        d_kv_raw[half:], "seq", [(i, i - SIDE) for i in range(SIDE, seqs)]
    )
    down_parts[0] = tie(down_parts[0], gate_up_sum)
    block_out = (resid + sum_parts(down_parts)).astype(BF16)
    attn_sum = added(attn_keep, tie(attn_got, gate_up_sum, block_out)).reshape(4, 2, shard, -1)
    attn_parts = send_along_z(attn_sum, mine)
    gate_up_share = added(take(gate_up_sum, x, 0), tie(gate_up_got, attn_sum))
    gate_up_other = swap(gate_up_share, "seq", SIDE)
    attn_parts[0] = tie(attn_parts[0], gate_up_share)
    attn_sum = added(*attn_parts)
    attn_got = swap(take(attn_sum, 1 - x, 0), "dp", 2)
    d_kv = added(d_kv_raw[:half], tie(from_later, attn_sum))
    d_qkv = jnp.concatenate([d_q_raw, d_kv], axis=1)
    d_normed_part = right_dot(d_qkv, w_qkv).astype(BF16)
    d_normed_parts = scatter_rows(d_normed_part)
    gate_up_share = added(gate_up_share, tie(gate_up_other, d_normed_part))
    gate_up_parts = gather_side(gate_up_share)
    attn_share = added(take(attn_sum, x, 0), tie(attn_got, gate_up_share))
    attn_other = swap(attn_share, "seq", SIDE)
    attn_share = added(attn_share, tie(attn_other, gate_up_share))
    attn_parts = gather_side(attn_share)
    d_normed_parts[0] = tie(d_normed_parts[0], attn_share)
    d_normed = sum_parts(d_normed_parts)
    normal1, inverse1 = norm_parts(states)
    grad_inputs = d_resid + norm_back(d_normed * attn_g, normal1, inverse1)

    outs = pl.pallas_call(
        functools.partial(place_kernel, piece, dps),
        out_shape=(
            out(shard, H * HD),
            out(shard, KV * HD),
            out(shard, KV * HD),
            out(shard, width),
            out(shard, ff),
            out(shard, ff),
            out(SIDE * piece, width),
            out(shard, 128),
        ),
        in_specs=[smem] + whole(2 * SIDE + 5),
        out_specs=tuple(whole(8)),
        scratch_shapes=[
            pltpu.VMEM((SIDE,) + gate_up_share.shape, BF16),
            pltpu.VMEM((SIDE,) + attn_share.shape, BF16),
        ],
        compiler_params=params,
    )(
        side_ref,
        *gate_up_parts,
        *attn_parts,
        w_query,
        w_key,
        w_value,
        w_gate,
        w_up,
    )
    out_query, out_key, out_value, out_out, out_gate, out_up, out_down, out_gains = outs
    return (
        block_out[None],
        grad_inputs[None],
        out_query,
        out_key,
        out_value,
        out_out,
        out_gate,
        out_up,
        out_down,
        out_gains[:, 2] / attn_gain.astype(F32),
        out_gains[:, 3] / ffn_gain.astype(F32),
        out_gains[:few, 0],
        out_gains[:few, 1],
    )


def solution(mesh):
    tokens = P("dp", "seq", None)
    weight = P("dp", None)
    gain = P("dp")
    return jax.shard_map(
        shards,
        mesh=mesh,
        in_specs=(tokens, P("dp", "seq")) + (weight,) * 7 + (gain,) * 4 + (tokens,),
        out_specs=(tokens, tokens) + (weight,) * 7 + (gain,) * 4,
        check_vma=False,
    )
```

```python
import functools

import jax
import jax.numpy as jnp
from jax import lax
from jax.experimental import pallas as pl
from jax.experimental.pallas import tpu as pltpu
from jax.sharding import PartitionSpec as P

H = 16
KV = 8
HD = 64
SIDE = 4

EPS = 1e-05
BASE = 1000000.0
MASKED = -1e30
SCALE = HD ** (-0.5)
BF16 = jnp.bfloat16
F32 = jnp.float32
VMEM_LIMIT = 50 * 1024 * 1024


def left_dot(left, right):
    return lax.dot_general(left, right, (((0,), (0,)), ((), ())), preferred_element_type=F32)


def right_dot(left, right):
    return lax.dot_general(left, right, (((1,), (1,)), ((), ())), preferred_element_type=F32)


def dot(left, right):
    return lax.dot_general(left, right, (((1,), (0,)), ((), ())), preferred_element_type=F32)


def norm_parts(values):
    inverse = lax.rsqrt(jnp.mean(values * values, axis=-1, keepdims=True) + EPS)
    return (values * inverse, inverse)


def norm_back(incoming, normal, inverse):
    return inverse * (incoming - normal * jnp.mean(incoming * normal, axis=-1, keepdims=True))


def swap(block, axis, step):
    size = lax.axis_size(axis)
    return lax.ppermute(block, axis, [(i, i ^ step) for i in range(size)])


def gather_side(block):
    return [block] + [swap(block, "seq", k) for k in range(1, SIDE)]


def scatter_side(blocks):
    return [blocks[0]] + [swap(blocks[k], "seq", k) for k in range(1, SIDE)]


def tie(value, *after):
    return lax.optimization_barrier((value,) + after)[0]


def take(array, index, axis):
    return lax.dynamic_index_in_dim(array, index, axis=axis, keepdims=False)


def added(*pieces):
    return sum(piece.astype(F32) for piece in pieces).astype(BF16)


def send_along_z(total, mine):
    z = mine >> 2
    return [take(total, z, 0)] + [swap(take(total, z ^ k, 0), "dp", 4 * k) for k in range(1, 4)]


def whole(count):
    return [pl.BlockSpec(memory_space=pltpu.VMEM)] * count


def lanes(shape):
    return lax.broadcasted_iota(jnp.int32, shape, len(shape) - 1)


def head_mean(values):
    row = lax.broadcasted_iota(jnp.int32, (128, 128), 0)
    ones = jnp.where(row // HD == lanes((128, 128)) // HD, 1.0 / HD, 0.0).astype(BF16)
    high = values.astype(BF16)
    rest = (values - high.astype(F32)).astype(BF16)
    return dot(high, ones) + dot(rest, ones)


def partner(values):
    return jnp.where(
        lanes(values.shape) % HD < HD // 2,
        pltpu.roll(values, 128 - HD // 2, 1),
        pltpu.roll(values, HD // 2, 1),
    )


def doubled(pair, head):
    other = pltpu.roll(pair.astype(F32), HD, 1).astype(pair.dtype)
    first = lanes(pair.shape) < HD
    return jnp.where(first, pair, other) if head == 0 else jnp.where(first, other, pair)


def two_heads(block):
    first = lanes(block.shape) < HD
    zero = jnp.zeros_like(block)
    return jnp.concatenate([jnp.where(first, block, zero), jnp.where(first, zero, block)], axis=0)


def sublanes(shape):
    return lax.broadcasted_iota(jnp.int32, shape, len(shape) - 2)


def pack_kernel(few, where, query, key, value, out_weight, gains, pack, scratch, sems):
    side, mine = where[0], where[1]
    shard, width = out_weight.shape
    copies = []
    begin = 0
    for weight in (query, key, value):
        count = weight.shape[1] // SIDE
        at = pl.ds(pl.multiple_of(side * count, count), count)
        copies.append((weight.at[:, at], pack.at[pl.ds(0, shard), pl.ds(begin, count)]))
        begin += count
    copies.append((out_weight, pack.at[pl.ds(0, shard), pl.ds(begin, width)]))
    copies = [
        pltpu.make_async_copy(source, target, sems.at[index])
        for index, (source, target) in enumerate(copies)
    ]
    for copy in copies:
        copy.start()

    def spread(gain, count, lane_count):
        row = jnp.concatenate([gain] * (lane_count // count), axis=1)
        return row, lanes(row.shape)

    all_gains = gains[...].astype(F32)
    rows = []
    for gain in (all_gains[:, :shard], all_gains[:, shard : 2 * shard]):
        row, lane = spread(gain, shard, width)
        rows.append(jnp.where(lane // shard == mine, row, 0.0))
    for index in range(2):
        gain = all_gains[:, 2 * shard + index * few : 2 * shard + (index + 1) * few]
        row, lane = spread(gain, few, 128)
        row = jnp.where(lane % HD // few == mine, row, 0.0)
        rows.append(jnp.concatenate([row, jnp.zeros((1, width - 128), F32)], axis=1))
    at = sublanes((16, width))
    extra = jnp.zeros((16, width), F32)
    for index, row in enumerate(rows):
        extra = jnp.where(at == index, row, extra)
    extra = jnp.concatenate([extra, jnp.zeros((16, begin), F32)], axis=1)
    scratch[...] = extra.astype(BF16)
    last = pltpu.make_async_copy(scratch, pack.at[pl.ds(shard, 16), :], sems.at[len(copies)])
    last.start()
    for copy in copies + [last]:
        copy.wait()


def start_of(place, cuts):
    return jnp.where(place >= cuts[1], cuts[1], jnp.where(place >= cuts[0], cuts[0], 0.0))


def forward_kernel(parts, me, *refs):
    token_refs = refs[:parts]
    packed, cos_table, sin_table = refs[parts : parts + 3]
    normed_out, q_raw, k_raw, query, key, value, mixed, gains = refs[parts + 3 : parts + 11]
    cosine, sine, bounds, k_two, v_two = refs[parts + 11 :]
    rows = query.shape[0] // SIDE
    width = token_refs[0].shape[1]
    q_cols = query.shape[1]
    cols = q_cols + 2 * key.shape[1]
    shard = packed.shape[1] - 16
    weight = packed[:, :shard, :cols].reshape(width, cols)
    gains[...] = jnp.sum(packed[:, shard:, :width].astype(F32), axis=0)
    gain, q_gain, k_gain = gains[0:1, :], gains[2:3, :128], gains[3:4, :128]

    bases = [(me[0] ^ part) * rows for part in range(parts)]
    row_places = [(lanes((1, rows)) + base).astype(F32) for base in bases]
    cuts = []
    for number in (1.0, 2.0):
        least = jnp.full((1, rows), 4096.0, F32)
        for part in range(parts):
            ids = token_refs[part][rows:, :rows].astype(F32)[0:1]
            least = jnp.minimum(least, jnp.where(ids == number, row_places[part], 4096.0))
        cuts.append(jnp.min(least, axis=1, keepdims=True))
    for index in range(2):
        bounds[index : index + 1, :] = jnp.broadcast_to(cuts[index], (1, 128))
    at_cut = []
    all_places = sublanes(cos_table.shape).astype(F32)
    for cut in cuts:
        there = all_places == cut
        at_cut.append(
            [
                jnp.sum(jnp.where(there, table[...], 0.0), axis=0, keepdims=True)
                for table in (cos_table, sin_table)
            ]
        )
    sign = jnp.where(lanes((1, 128)) % HD < HD // 2, -1.0, 1.0)

    for part in range(parts):
        at = pl.ds(part * rows, rows)
        states = token_refs[part][:rows, :].astype(F32)
        inverse = lax.rsqrt(jnp.mean(states * states, axis=-1, keepdims=True) + EPS)
        normed = (states * inverse * gain).astype(BF16)
        there = pl.ds(pl.multiple_of(bases[part], rows), rows)
        place = (sublanes((rows, 128)) + bases[part]).astype(F32)
        cos_cut = jnp.where(
            place >= cuts[1], at_cut[1][0], jnp.where(place >= cuts[0], at_cut[0][0], 1.0)
        )
        sin_cut = jnp.where(
            place >= cuts[1], at_cut[1][1], jnp.where(place >= cuts[0], at_cut[0][1], 0.0)
        )
        cos = cos_table[there, :] * cos_cut + sin_table[there, :] * sin_cut
        sin = (sin_table[there, :] * cos_cut - cos_table[there, :] * sin_cut) * sign
        cosine[at, :] = cos
        sine[at, :] = sin
        normed_out[at, :] = normed
        if part < SIDE:
            raw = dot(normed, weight)
            raw_q, raw_kv = raw[:, :q_cols], raw[:, q_cols:]
            q_raw[at, :] = raw_q
            for pair in range(q_cols // 128):
                here = pl.ds(pair * 128, 128)
                one = raw_q[:, pair * 128 : (pair + 1) * 128]
                scaled = one * lax.rsqrt(head_mean(one * one) + EPS) * q_gain
                query[at, here] = (scaled * cos + partner(scaled) * sin).astype(BF16)
        else:
            raw_kv = dot(normed, weight[:, q_cols:])
        one = raw_kv[:, :128]
        k_raw[at, :] = one
        scaled = one * lax.rsqrt(head_mean(one * one) + EPS) * k_gain
        key[at, :] = (scaled * cos + partner(scaled) * sin).astype(BF16)
        value[at, :] = raw_kv[:, 128:].astype(BF16)
    k_place = jnp.concatenate(row_places, axis=1)
    for pair in range(q_cols // 128):
        here = pl.ds(pair * 128, 128)
        k_two[...] = doubled(key[...], pair)
        v_two[...] = doubled(value[...], pair)

        @pl.loop(0, SIDE)
        def _(step):
            at = pl.ds(pl.multiple_of(step * rows, rows), rows)
            q_place = (sublanes((rows, 1)) + (me[0] ^ step) * rows).astype(F32)
            q_place = jnp.concatenate([q_place, q_place], axis=0)
            allowed = (k_place <= q_place) & (k_place >= start_of(q_place, cuts))
            scores = right_dot(two_heads(query[at, here]), k_two[...]) * SCALE
            scores = jnp.where(allowed, scores, MASKED)
            expd = jnp.exp(scores - jnp.max(scores, axis=-1, keepdims=True))
            probs = (expd * (1.0 / jnp.sum(expd, axis=-1, keepdims=True))).astype(BF16)
            both = dot(probs, v_two[...])
            mixed[at, here] = jnp.where(
                lanes((rows, 128)) < HD, both[:rows], both[rows:]
            ).astype(BF16)


def backward_kernel(me, *refs):
    d_mixed, attended = refs[:SIDE], refs[SIDE : 2 * SIDE]
    query, key, value, q_raw, k_raw, cosine, sine, normed = refs[2 * SIDE : 2 * SIDE + 8]
    gains, bounds, d_q_raw, d_kv_raw, keep, send = refs[2 * SIDE + 8 : 2 * SIDE + 14]
    k_two, v_two, d_k, d_v, d_q, d_both, k_place, all_attended, d_cols = refs[2 * SIDE + 14 :]
    rows = d_mixed[0].shape[0]
    length = key.shape[0]
    q_cols = query.shape[1]
    pairs = q_cols // 128
    q_gain, k_gain = gains[2:3, :128], gains[3:4, :128]
    cuts = [bounds[0:1, :], bounds[1:2, :]]
    for part in range(SIDE):
        at = pl.ds(part * rows, rows)
        d_both[at, :] = d_mixed[part][:, :q_cols]
        d_cols[at, :] = d_mixed[part][:, q_cols:]
        all_attended[at, :] = attended[part][...]
    for part in range(length // rows):
        base = (me[0] ^ part) * rows
        k_place[pl.ds(part * rows, rows), :] = (sublanes((rows, 128)) + base).astype(F32)
    for pair in range(pairs):
        here = pl.ds(pair * 128, 128)
        k_two[...] = doubled(key[...], pair)
        v_two[...] = doubled(value[...], pair)
        d_k[pair] = jnp.zeros((length, 128), F32)
        d_v[pair] = jnp.zeros((length, 128), F32)

        @pl.loop(0, SIDE)
        def _(step):
            at = pl.ds(pl.multiple_of(step * rows, rows), rows)
            q_place = (lanes((1, rows)) + (me[0] ^ step) * rows).astype(F32)
            allowed = (k_place[...] <= q_place) & (k_place[...] >= start_of(q_place, cuts))
            allowed = jnp.concatenate([allowed, allowed], axis=1)
            q_two = two_heads(query[at, here])
            d_two = two_heads(d_both[at, here])
            scores = jnp.where(allowed, right_dot(k_two[...], q_two) * SCALE, MASKED)
            expd = jnp.exp(scores - jnp.max(scores, axis=0, keepdims=True))
            probs = expd * (1.0 / jnp.sum(expd, axis=0, keepdims=True))
            d_probs = right_dot(v_two[...], d_two)
            delta = jnp.sum(probs * d_probs, axis=0, keepdims=True)
            d_scores = (probs * (d_probs - delta)).astype(BF16)
            d_v[pair] += dot(probs.astype(BF16), d_two)
            d_k[pair] += dot(d_scores, q_two)
            both = left_dot(d_scores, k_two[...])
            d_q[at, here] = jnp.where(lanes((rows, 128)) < HD, both[:rows], both[rows:]) * SCALE

    first = lanes((rows, 128)) < HD
    sums = [jnp.zeros((1, 128), F32), jnp.zeros((1, 128), F32)]

    def back(incoming, raw, gain, at, which):
        inverse = lax.rsqrt(head_mean(raw * raw) + EPS)
        normal = raw * inverse
        incoming = incoming.astype(BF16).astype(F32)
        turned = incoming * cosine[at, :] - partner(incoming) * sine[at, :]
        sums[which] = sums[which] + jnp.sum(turned * normal, axis=0, keepdims=True)
        turned = turned * gain
        return (inverse * (turned - normal * head_mean(turned * normal))).astype(BF16)

    def joined(pieces):
        pieces = [piece + pltpu.roll(piece, HD, 1) for piece in pieces]
        return jnp.where(first, pieces[0], pieces[1])

    for part in range(length // rows):
        at = pl.ds(part * rows, rows)
        if part < SIDE:
            for pair in range(pairs):
                here = pl.ds(pair * 128, 128)
                d_q_raw[at, here] = back(d_q[at, here], q_raw[at, here], q_gain, at, 0)
        d_key = joined([d_k[pair, at, :] for pair in range(pairs)]) * SCALE
        d_kv_raw[at, :128] = back(d_key, k_raw[at, :], k_gain, at, 1)
        d_kv_raw[at, 128:] = joined([d_v[pair, at, :] for pair in range(pairs)]).astype(BF16)

    half = SIDE * rows
    width = normed.shape[1]
    shard = HD
    few = HD * shard // width
    sums = [total + pltpu.roll(total, HD, 1) for total in sums]
    row, lane = sublanes((8, 128)), lanes((8, 128))

    def gain_block(p):
        there = (row < few) & (lane == p * few + row)
        sides = [jnp.sum(jnp.where(there, total, 0.0), axis=1, keepdims=True) for total in sums]
        block = jnp.where(lane == 0, sides[0], jnp.where(lane == 1, sides[1], 0.0))
        return jnp.concatenate([block, jnp.zeros((shard - 8, 128), F32)], axis=0)

    first_core = me[1] == 0
    for chunk in range(width // 256):
        here = pl.ds(chunk * 256, 256)
        terms = jnp.concatenate(
            [
                left_dot(normed[:half, here], d_q_raw[...]),
                left_dot(normed[:, here], d_kv_raw[...]),
                left_dot(all_attended[:, here], d_cols[...]),
            ],
            axis=1,
        )
        for pair in range(256 // (2 * shard)):
            blocks = []
            for core in range(2):
                begin = (2 * pair + core) * shard
                p = begin // shard + chunk * (256 // shard)
                blocks.append(
                    jnp.concatenate([terms[begin : begin + shard], gain_block(p)], axis=1)
                )
            at = pl.ds((chunk * (256 // shard) // 2 + pair) * shard, shard)
            keep[at, :] = jnp.where(first_core, blocks[0], blocks[1]).astype(BF16)
            send[at, :] = jnp.where(first_core, blocks[1], blocks[0]).astype(BF16)


def terms_kernel(where, tokens, d_gate, d_up, hidden, cot, down, keep, send, out_part, grad_down):
    first_core = where[1] == 0
    shard = HD
    cols = d_gate.shape[1]
    tall = keep.shape[0] // 8
    width = tokens.shape[1]
    piece = hidden.shape[1] // 16
    wide = 2 * cols - 2 * width

    def store(block, begin, here, one, two):
        at = pl.ds(block * tall + begin, one.shape[0])
        keep[at, here] = jnp.where(first_core, one, two).astype(BF16)
        send[at, here] = jnp.where(first_core, two, one).astype(BF16)

    for chunk in range(width // 256):
        left = tokens[:, chunk * 256 : (chunk + 1) * 256]
        for which, right in enumerate((d_gate, d_up)):
            here = pl.ds(which * cols, cols)
            terms = left_dot(left, right[...]).reshape(2, 2, shard, cols)
            for pair in range(2):
                store(chunk * 2 + pair, 0, here, terms[pair, 0], terms[pair, 1])
    for chunk in range(hidden.shape[1] // 384):
        here = pl.ds(chunk * 384, 384)
        grad_down[here, :] = left_dot(hidden[:, here], cot[...])

    def folded(p):
        rows = grad_down[p * piece : (p + 1) * piece, :]
        rest = [rows[64:, j * wide : (j + 1) * wide] for j in range(width // wide)]
        return jnp.concatenate([rows[:32], rows[32:64], jnp.concatenate(rest, axis=0)], axis=1)

    for block in range(8):
        store(block, shard, pl.ds(0, 2 * cols), folded(2 * block), folded(2 * block + 1))
    for chunk in range(hidden.shape[0] // 128):
        at = pl.ds(chunk * 128, 128)
        out_part[at, :] = dot(hidden[at, :], down[...]).astype(BF16)


def pick_kernel(piece, side, gate, up, out):
    for j in range(SIDE):

        @pl.when(side[0] == j)
        def _():
            pieces = []
            for weight in (gate, up):
                values = weight[...].astype(F32)
                for begin in range(j * piece, values.shape[1], SIDE * piece):
                    pieces.append(values[:, begin : begin + piece])
            out[...] = jnp.concatenate(pieces, axis=1).astype(BF16)


def place_kernel(piece, shards_count, *refs):
    side = refs[0]
    big, small = refs[1 : 1 + SIDE], refs[1 + SIDE : 1 + 2 * SIDE]
    weights = refs[1 + 2 * SIDE : 6 + 2 * SIDE]
    outs = refs[6 + 2 * SIDE : -2]
    big_all, small_all = refs[-2:]
    for k in range(SIDE):
        big_all[side[0] ^ k] = big[k][...]
        small_all[side[0] ^ k] = small[k][...]
    out_query, out_key, out_value, out_out, out_gate, out_up, out_down, out_gains = outs
    shard = out_gate.shape[0]
    ff_cols = piece * shards_count
    for j in range(SIDE):
        mine = small_all[j].astype(F32)
        begin = 0
        for out in (out_query, out_key, out_value, out_out):
            count = out.shape[1] // SIDE
            out[:, j * count : (j + 1) * count] = mine[:, begin : begin + count]
            begin += count
        out_gains[...] = mine[:, begin:] if j == 0 else out_gains[...] + mine[:, begin:]
        folded = big_all[j, shard:, :].astype(F32)
        width = out_down.shape[1]
        out_down[j * piece : j * piece + 32, :] = folded[:, :width]
        out_down[j * piece + 32 : j * piece + 64, :] = folded[:, width : 2 * width]
        rest = [folded[8 * i : 8 * i + 8, 2 * width :] for i in range(4)]
        out_down[j * piece + 64 : (j + 1) * piece, :] = jnp.concatenate(rest, axis=1)
    for which, out in enumerate((out_gate, out_up)):
        pieces = []
        both = [
            big_all[j, :shard, which * ff_cols : (which + 1) * ff_cols].astype(F32)
            for j in range(SIDE)
        ]
        for p in range(shards_count):
            for j in range(SIDE):
                pieces.append(both[j][:, p * piece : (p + 1) * piece])
        out[...] = jnp.concatenate(pieces, axis=1)

    def products(pairs):
        return sum(
            jnp.sum(out[...] * weight[...].astype(F32), axis=1, keepdims=True)
            for out, weight in pairs
        )

    attn = products(zip((out_query, out_key, out_value), weights[:3]))
    ffn = products(zip((out_gate, out_up), weights[3:]))
    lane = lanes(out_gains.shape)
    out_gains[...] = jnp.where(lane == 2, attn, jnp.where(lane == 3, ffn, out_gains[...]))


def shards(
    inputs,
    doc_ids,
    w_query,
    w_key,
    w_value,
    w_out,
    w_gate,
    w_up,
    w_down,
    attn_gain,
    ffn_gain,
    query_gain,
    key_gain,
    cotangent,
):
    rows, width = inputs.shape[1:]
    seqs = lax.axis_size("seq")
    dps = lax.axis_size("dp")
    me = lax.axis_index("seq").astype(jnp.uint32)
    side = me & (SIDE - 1)
    length = rows * seqs
    half = rows * SIDE
    shard = w_query.shape[0]
    q_cols = H * HD // SIDE
    kv_cols = KV * HD // SIDE
    ff = w_gate.shape[1]
    ff_cols = ff // SIDE
    piece = w_down.shape[0] // SIDE
    tall = max(piece, shard)
    cols = q_cols + 2 * kv_cols

    def columns(weight, count):
        return lax.dynamic_slice_in_dim(weight, side * count, count, axis=1)

    def out(*shape, dtype=F32):
        return jax.ShapeDtypeStruct(shape, dtype)

    params = pltpu.CompilerParams(vmem_limit_bytes=VMEM_LIMIT)

    tokens = inputs[0]
    cot = cotangent[0]
    mine = lax.axis_index("dp").astype(jnp.uint32)
    core, x, z = mine & 1, (mine >> 1) & 1, mine >> 2
    few = HD // dps
    smem = pl.BlockSpec(memory_space=pltpu.SMEM)
    me_ref = me.astype(jnp.int32).reshape(1)
    attn_pack = pl.pallas_call(
        functools.partial(pack_kernel, few),
        out_shape=out(shard + 16, cols + width, dtype=BF16),
        in_specs=[smem] + [pl.BlockSpec(memory_space=pltpu.HBM)] * 4 + whole(1),
        out_specs=pl.BlockSpec(memory_space=pl.ANY),
        scratch_shapes=[pltpu.VMEM((16, cols + width), BF16), pltpu.SemaphoreType.DMA((5,))],
        compiler_params=params,
    )(
        jnp.stack([side, mine]).astype(jnp.int32),
        w_query,
        w_key,
        w_value,
        w_out,
        jnp.concatenate([attn_gain, ffn_gain, query_gain, key_gain])[None],
    )
    attn_all = lax.all_gather(attn_pack, "dp", axis=0, tiled=False)
    ids = jnp.pad(doc_ids.astype(BF16), ((0, 15), (0, width - rows)))
    message = jnp.concatenate([tokens, ids], axis=0)
    token_parts = [message] + [swap(message, "seq", k) for k in range(1, SIDE)]
    earlier = lax.ppermute(message, "seq", [(i, i ^ SIDE) for i in range(SIDE)])
    token_parts.append(earlier)
    for k in range(1, SIDE):
        token_parts.append(lax.ppermute(earlier, "seq", [(i, i ^ k) for i in range(SIDE, seqs)]))
    cot_parts = gather_side(cot)

    side_ref = side.astype(jnp.int32).reshape(1)
    picked = pl.pallas_call(
        functools.partial(pick_kernel, piece),
        out_shape=out(shard, 2 * ff_cols, dtype=BF16),
        in_specs=[smem] + whole(2),
        out_specs=whole(1)[0],
        compiler_params=params,
    )(side_ref, w_gate, w_up)
    down_piece = lax.dynamic_slice_in_dim(w_down, side * piece, piece, axis=0)
    pack = jnp.concatenate(
        [
            jnp.pad(picked, ((0, tall - shard), (0, 0))),
            jnp.pad(down_piece, ((0, tall - piece), (0, 0))),
        ],
        axis=1,
    )
    packed = lax.all_gather(pack, "dp", axis=0, tiled=False)
    w_qkv = attn_all[:, :shard, :cols].reshape(width, cols)
    wo = attn_all[:, :shard, cols:].reshape(H * HD, width)
    w_gate_up = packed[:, :shard, : 2 * ff_cols].reshape(width, 2 * ff_cols)
    wd = packed[:, :piece, 2 * ff_cols :].reshape(ff_cols, width)

    freqs = BASE ** (-(jnp.arange(HD // 2, dtype=F32) * (2.0 / HD)))
    freqs = jnp.concatenate([freqs] * 4)
    angles = jnp.arange(length, dtype=jnp.int32).astype(F32)[:, None] * freqs[None, :]

    normed, q_raw, k_raw, query, key, value, mixed, gains, cosine, sine, bounds = pl.pallas_call(
        functools.partial(forward_kernel, seqs),
        out_shape=(
            out(length, width, dtype=BF16),
            out(half, q_cols),
            out(length, kv_cols),
            out(half, q_cols, dtype=BF16),
            out(length, kv_cols, dtype=BF16),
            out(length, kv_cols, dtype=BF16),
            out(half, q_cols, dtype=BF16),
            out(16, width),
            out(length, 128),
            out(length, 128),
            out(8, 128),
        ),
        in_specs=[smem] + whole(seqs + 3),
        out_specs=tuple(whole(11)),
        scratch_shapes=[pltpu.VMEM((length, 128), BF16)] * 2,
        compiler_params=params,
        cost_estimate=pl.CostEstimate(
            flops=10_000_000_000, bytes_accessed=10_000_000, transcendentals=2_000_000
        ),
    )(me_ref, *token_parts, attn_all, jnp.cos(angles), jnp.sin(angles))
    attn_g = gains[0:1]
    ffn_g = gains[1:2]

    mixed = tie(mixed, *cot_parts)
    mixed_parts = scatter_side([mixed[k * rows : (k + 1) * rows] for k in range(SIDE)])
    attended_parts = jnp.stack(mixed_parts)
    attended = jnp.concatenate(
        [
            lax.dynamic_index_in_dim(attended_parts, side ^ j, axis=0, keepdims=False)
            for j in range(SIDE)
        ],
        axis=1,
    )
    states = tokens.astype(F32)
    resid = states + dot(attended, wo)
    normal2, inverse2 = norm_parts(resid)
    normed2 = (normal2 * ffn_g).astype(BF16)

    normed2_all = jnp.concatenate(gather_side(tie(normed2, w_qkv)), axis=0)
    attended_parts = gather_side(tie(attended, normed2_all))
    cot_all = jnp.concatenate(cot_parts, axis=0)
    gate_up = dot(normed2_all, w_gate_up)
    gate, upper = gate_up[:, :ff_cols], gate_up[:, ff_cols:]
    d_hidden = right_dot(cot_all, wd)
    sigmoid_gate = jax.nn.sigmoid(gate)
    active = gate * sigmoid_gate
    hidden = (active * upper).astype(BF16)
    d_gate = d_hidden * upper * sigmoid_gate * (1.0 + gate * (1.0 - sigmoid_gate))
    d_upper = d_hidden * active
    d_gate, d_upper = d_gate.astype(BF16), d_upper.astype(BF16)
    d_gate_up = jnp.concatenate([d_gate, d_upper], axis=1)
    d_normed2_part = right_dot(d_gate_up, w_gate_up).astype(BF16)

    def scatter_rows(blocks):
        return scatter_side([blocks[k * rows : (k + 1) * rows] for k in range(SIDE)])

    def sum_parts(received):
        return sum(part.astype(F32) for part in received)

    d_normed2_parts = scatter_rows(d_normed2_part)

    where = jnp.stack([me, core]).astype(jnp.int32)
    gate_up_keep, gate_up_send, down_part = pl.pallas_call(
        terms_kernel,
        out_shape=(
            out(dps // 2 * (shard + 32), 2 * ff_cols, dtype=BF16),
            out(dps // 2 * (shard + 32), 2 * ff_cols, dtype=BF16),
            out(half, width, dtype=BF16),
        ),
        in_specs=[smem] + whole(6),
        out_specs=tuple(whole(3)),
        scratch_shapes=[pltpu.VMEM((ff_cols, width), F32)],
        compiler_params=params,
        cost_estimate=pl.CostEstimate(
            flops=10_000_000_000, bytes_accessed=20_000_000, transcendentals=0
        ),
    )(
        where,
        normed2_all,
        tie(d_gate, d_normed2_part, *attended_parts),
        d_upper,
        hidden,
        cot_all,
        wd,
    )
    d_normed2_parts[0] = tie(d_normed2_parts[0], down_part)
    d_normed2 = sum_parts(d_normed2_parts)
    gate_up_got = swap(tie(gate_up_send, d_normed2), "dp", 1)

    d_resid = cot.astype(F32) + norm_back(d_normed2 * ffn_g, normal2, inverse2)
    d_resid_low = d_resid.astype(BF16)
    d_attended = right_dot(d_resid_low, wo).astype(BF16)
    out_cols = width // SIDE
    d_messages = scatter_side(
        [
            jnp.concatenate(
                [
                    lax.dynamic_slice_in_dim(d_attended, (side ^ k) * q_cols, q_cols, axis=1),
                    lax.dynamic_slice_in_dim(d_resid_low, (side ^ k) * out_cols, out_cols, axis=1),
                ],
                axis=1,
            )
            for k in range(SIDE)
        ]
    )
    gate_up_sum = added(gate_up_keep, tie(gate_up_got, d_attended))
    gate_up_parts = send_along_z(gate_up_sum.reshape(4, 2, shard + 32, -1), mine)
    down_parts = scatter_rows(tie(down_part, *d_messages))

    d_q_raw, d_kv_raw, attn_keep, attn_send = pl.pallas_call(
        backward_kernel,
        out_shape=(
            out(half, q_cols, dtype=BF16),
            out(length, 2 * kv_cols, dtype=BF16),
            out(width // 2, cols + out_cols + 128, dtype=BF16),
            out(width // 2, cols + out_cols + 128, dtype=BF16),
        ),
        in_specs=[smem] + whole(2 * SIDE + 10),
        out_specs=tuple(whole(4)),
        scratch_shapes=[
            pltpu.VMEM((length, 128), BF16),
            pltpu.VMEM((length, 128), BF16),
            pltpu.VMEM((2, length, 128), F32),
            pltpu.VMEM((2, length, 128), F32),
            pltpu.VMEM((half, q_cols), F32),
            pltpu.VMEM((half, q_cols), BF16),
            pltpu.VMEM((length, 128), F32),
            pltpu.VMEM((half, width), BF16),
            pltpu.VMEM((half, out_cols), BF16),
        ],
        compiler_params=params,
        cost_estimate=pl.CostEstimate(
            flops=14_000_000_000, bytes_accessed=10_000_000, transcendentals=2_000_000
        ),
    )(
        where,
        *d_messages,
        *attended_parts,
        query,
        key,
        value,
        q_raw,
        k_raw,
        cosine,
        sine,
        normed,
        gains,
        bounds,
    )
    attn_got = swap(attn_send, "dp", 1)
    from_later = lax.ppermute(
        d_kv_raw[half:], "seq", [(i, i - SIDE) for i in range(SIDE, seqs)]
    )
    attn_sum = added(attn_keep, attn_got)
    attn_parts = send_along_z(attn_sum.reshape(4, 2, shard, -1), mine)
    d_kv = added(d_kv_raw[:half], tie(from_later, attn_sum))
    d_qkv = jnp.concatenate([d_q_raw, d_kv], axis=1)
    d_normed_part = right_dot(d_qkv, w_qkv).astype(BF16)
    d_normed_parts = scatter_rows(d_normed_part)
    down_parts[0] = tie(down_parts[0], d_normed_part)
    block_out = (resid + sum_parts(down_parts)).astype(BF16)
    gate_up_parts[0] = tie(gate_up_parts[0], block_out)
    gate_up_sum = added(*gate_up_parts)
    gate_up_got = swap(take(gate_up_sum, 1 - x, 0), "dp", 2)
    attn_parts[0] = tie(attn_parts[0], gate_up_sum)
    attn_sum = added(*attn_parts)
    attn_got = swap(take(attn_sum, 1 - x, 0), "dp", 2)
    gate_up_share = added(take(gate_up_sum, x, 0), tie(gate_up_got, attn_sum))
    gate_up_other = swap(gate_up_share, "seq", SIDE)
    attn_share = added(take(attn_sum, x, 0), tie(attn_got, gate_up_share))
    attn_other = swap(attn_share, "seq", SIDE)
    gate_up_share = added(gate_up_share, tie(gate_up_other, attn_share))
    gate_up_parts = gather_side(gate_up_share)
    attn_share = added(attn_share, tie(attn_other, gate_up_share))
    attn_parts = gather_side(attn_share)
    d_normed_parts[0] = tie(d_normed_parts[0], attn_share)
    d_normed = sum_parts(d_normed_parts)
    normal1, inverse1 = norm_parts(states)
    grad_inputs = d_resid + norm_back(d_normed * attn_g, normal1, inverse1)

    outs = pl.pallas_call(
        functools.partial(place_kernel, piece, dps),
        out_shape=(
            out(shard, H * HD),
            out(shard, KV * HD),
            out(shard, KV * HD),
            out(shard, width),
            out(shard, ff),
            out(shard, ff),
            out(SIDE * piece, width),
            out(shard, 128),
        ),
        in_specs=[smem] + whole(2 * SIDE + 5),
        out_specs=tuple(whole(8)),
        scratch_shapes=[
            pltpu.VMEM((SIDE,) + gate_up_share.shape, BF16),
            pltpu.VMEM((SIDE,) + attn_share.shape, BF16),
        ],
        compiler_params=params,
    )(
        side_ref,
        *gate_up_parts,
        *attn_parts,
        w_query,
        w_key,
        w_value,
        w_gate,
        w_up,
    )
    out_query, out_key, out_value, out_out, out_gate, out_up, out_down, out_gains = outs
    return (
        block_out[None],
        grad_inputs[None],
        out_query,
        out_key,
        out_value,
        out_out,
        out_gate,
        out_up,
        out_down,
        out_gains[:, 2] / attn_gain.astype(F32),
        out_gains[:, 3] / ffn_gain.astype(F32),
        out_gains[:few, 0],
        out_gains[:few, 1],
    )


def solution(mesh):
    tokens = P("dp", "seq", None)
    weight = P("dp", None)
    gain = P("dp")
    return jax.shard_map(
        shards,
        mesh=mesh,
        in_specs=(tokens, P("dp", "seq")) + (weight,) * 7 + (gain,) * 4 + (tokens,),
        out_specs=(tokens, tokens) + (weight,) * 7 + (gain,) * 4,
        check_vma=False,
    )
```

```python
import functools

import jax
import jax.numpy as jnp
from jax import lax
from jax.experimental import pallas as pl
from jax.experimental.pallas import tpu as pltpu
from jax.sharding import PartitionSpec as P

H = 16
KV = 8
HD = 64
SIDE = 4

EPS = 1e-05
BASE = 1000000.0
MASKED = -1e30
SCALE = HD ** (-0.5)
BF16 = jnp.bfloat16
F32 = jnp.float32
VMEM_LIMIT = 50 * 1024 * 1024


def left_dot(left, right):
    return lax.dot_general(left, right, (((0,), (0,)), ((), ())), preferred_element_type=F32)


def right_dot(left, right):
    return lax.dot_general(left, right, (((1,), (1,)), ((), ())), preferred_element_type=F32)


def dot(left, right):
    return lax.dot_general(left, right, (((1,), (0,)), ((), ())), preferred_element_type=F32)


def norm_parts(values):
    inverse = lax.rsqrt(jnp.mean(values * values, axis=-1, keepdims=True) + EPS)
    return (values * inverse, inverse)


def norm_back(incoming, normal, inverse):
    return inverse * (incoming - normal * jnp.mean(incoming * normal, axis=-1, keepdims=True))


def swap(block, axis, step):
    size = lax.axis_size(axis)
    return lax.ppermute(block, axis, [(i, i ^ step) for i in range(size)])


def gather_side(block):
    return [block] + [swap(block, "seq", k) for k in range(1, SIDE)]


def scatter_side(blocks):
    return [blocks[0]] + [swap(blocks[k], "seq", k) for k in range(1, SIDE)]


def tie(value, *after):
    return lax.optimization_barrier((value,) + after)[0]


def take(array, index, axis):
    return lax.dynamic_index_in_dim(array, index, axis=axis, keepdims=False)


def added(*pieces):
    return sum(piece.astype(F32) for piece in pieces).astype(BF16)


def send_along_z(total, mine):
    z = mine >> 2
    return [take(total, z, 0)] + [swap(take(total, z ^ k, 0), "dp", 4 * k) for k in range(1, 4)]


def whole(count):
    return [pl.BlockSpec(memory_space=pltpu.VMEM)] * count


def lanes(shape):
    return lax.broadcasted_iota(jnp.int32, shape, len(shape) - 1)


def head_mean(values):
    row = lax.broadcasted_iota(jnp.int32, (128, 128), 0)
    ones = jnp.where(row // HD == lanes((128, 128)) // HD, 1.0 / HD, 0.0).astype(BF16)
    high = values.astype(BF16)
    rest = (values - high.astype(F32)).astype(BF16)
    return dot(high, ones) + dot(rest, ones)


def partner(values):
    return jnp.where(
        lanes(values.shape) % HD < HD // 2,
        pltpu.roll(values, 128 - HD // 2, 1),
        pltpu.roll(values, HD // 2, 1),
    )


def doubled(pair, head):
    other = pltpu.roll(pair.astype(F32), HD, 1).astype(pair.dtype)
    first = lanes(pair.shape) < HD
    return jnp.where(first, pair, other) if head == 0 else jnp.where(first, other, pair)


def two_heads(block):
    first = lanes(block.shape) < HD
    zero = jnp.zeros_like(block)
    return jnp.concatenate([jnp.where(first, block, zero), jnp.where(first, zero, block)], axis=0)


def sublanes(shape):
    return lax.broadcasted_iota(jnp.int32, shape, len(shape) - 2)


def pack_kernel(few, where, query, key, value, out_weight, gains, pack, scratch, sems):
    side, mine = where[0], where[1]
    shard, width = out_weight.shape
    copies = []
    begin = 0
    for weight in (query, key, value):
        count = weight.shape[1] // SIDE
        at = pl.ds(pl.multiple_of(side * count, count), count)
        copies.append((weight.at[:, at], pack.at[pl.ds(0, shard), pl.ds(begin, count)]))
        begin += count
    copies.append((out_weight, pack.at[pl.ds(0, shard), pl.ds(begin, width)]))
    copies = [
        pltpu.make_async_copy(source, target, sems.at[index])
        for index, (source, target) in enumerate(copies)
    ]
    for copy in copies:
        copy.start()

    def spread(gain, count, lane_count):
        row = jnp.concatenate([gain] * (lane_count // count), axis=1)
        return row, lanes(row.shape)

    all_gains = gains[...].astype(F32)
    rows = []
    for gain in (all_gains[:, :shard], all_gains[:, shard : 2 * shard]):
        row, lane = spread(gain, shard, width)
        rows.append(jnp.where(lane // shard == mine, row, 0.0))
    for index in range(2):
        gain = all_gains[:, 2 * shard + index * few : 2 * shard + (index + 1) * few]
        row, lane = spread(gain, few, 128)
        row = jnp.where(lane % HD // few == mine, row, 0.0)
        rows.append(jnp.concatenate([row, jnp.zeros((1, width - 128), F32)], axis=1))
    at = sublanes((16, width))
    extra = jnp.zeros((16, width), F32)
    for index, row in enumerate(rows):
        extra = jnp.where(at == index, row, extra)
    extra = jnp.concatenate([extra, jnp.zeros((16, begin), F32)], axis=1)
    scratch[...] = extra.astype(BF16)
    last = pltpu.make_async_copy(scratch, pack.at[pl.ds(shard, 16), :], sems.at[len(copies)])
    last.start()
    for copy in copies + [last]:
        copy.wait()


def start_of(place, cuts):
    return jnp.where(place >= cuts[1], cuts[1], jnp.where(place >= cuts[0], cuts[0], 0.0))


def forward_kernel(parts, me, *refs):
    token_refs = refs[:parts]
    packed, cos_table, sin_table = refs[parts : parts + 3]
    normed_out, q_raw, k_raw, query, key, value, mixed, gains = refs[parts + 3 : parts + 11]
    cosine, sine, bounds, k_two, v_two = refs[parts + 11 :]
    rows = query.shape[0] // SIDE
    width = token_refs[0].shape[1]
    q_cols = query.shape[1]
    cols = q_cols + 2 * key.shape[1]
    shard = packed.shape[1] - 16
    weight = packed[:, :shard, :cols].reshape(width, cols)
    gains[...] = jnp.sum(packed[:, shard:, :width].astype(F32), axis=0)
    gain, q_gain, k_gain = gains[0:1, :], gains[2:3, :128], gains[3:4, :128]

    bases = [(me[0] ^ part) * rows for part in range(parts)]
    row_places = [(lanes((1, rows)) + base).astype(F32) for base in bases]
    cuts = []
    for number in (1.0, 2.0):
        least = jnp.full((1, rows), 4096.0, F32)
        for part in range(parts):
            ids = token_refs[part][rows:, :rows].astype(F32)[0:1]
            least = jnp.minimum(least, jnp.where(ids == number, row_places[part], 4096.0))
        cuts.append(jnp.min(least, axis=1, keepdims=True))
    for index in range(2):
        bounds[index : index + 1, :] = jnp.broadcast_to(cuts[index], (1, 128))
    at_cut = []
    all_places = sublanes(cos_table.shape).astype(F32)
    for cut in cuts:
        there = all_places == cut
        at_cut.append(
            [
                jnp.sum(jnp.where(there, table[...], 0.0), axis=0, keepdims=True)
                for table in (cos_table, sin_table)
            ]
        )
    sign = jnp.where(lanes((1, 128)) % HD < HD // 2, -1.0, 1.0)

    for part in range(parts):
        at = pl.ds(part * rows, rows)
        states = token_refs[part][:rows, :].astype(F32)
        inverse = lax.rsqrt(jnp.mean(states * states, axis=-1, keepdims=True) + EPS)
        normed = (states * inverse * gain).astype(BF16)
        there = pl.ds(pl.multiple_of(bases[part], rows), rows)
        place = (sublanes((rows, 128)) + bases[part]).astype(F32)
        cos_cut = jnp.where(
            place >= cuts[1], at_cut[1][0], jnp.where(place >= cuts[0], at_cut[0][0], 1.0)
        )
        sin_cut = jnp.where(
            place >= cuts[1], at_cut[1][1], jnp.where(place >= cuts[0], at_cut[0][1], 0.0)
        )
        cos = cos_table[there, :] * cos_cut + sin_table[there, :] * sin_cut
        sin = (sin_table[there, :] * cos_cut - cos_table[there, :] * sin_cut) * sign
        cosine[at, :] = cos
        sine[at, :] = sin
        normed_out[at, :] = normed
        if part < SIDE:
            raw = dot(normed, weight)
            raw_q, raw_kv = raw[:, :q_cols], raw[:, q_cols:]
            q_raw[at, :] = raw_q
            for pair in range(q_cols // 128):
                here = pl.ds(pair * 128, 128)
                one = raw_q[:, pair * 128 : (pair + 1) * 128]
                scaled = one * lax.rsqrt(head_mean(one * one) + EPS) * q_gain
                query[at, here] = (scaled * cos + partner(scaled) * sin).astype(BF16)
        else:
            raw_kv = dot(normed, weight[:, q_cols:])
        one = raw_kv[:, :128]
        k_raw[at, :] = one
        scaled = one * lax.rsqrt(head_mean(one * one) + EPS) * k_gain
        key[at, :] = (scaled * cos + partner(scaled) * sin).astype(BF16)
        value[at, :] = raw_kv[:, 128:].astype(BF16)
    k_place = jnp.concatenate(row_places, axis=1)
    for pair in range(q_cols // 128):
        here = pl.ds(pair * 128, 128)
        k_two[...] = doubled(key[...], pair)
        v_two[...] = doubled(value[...], pair)

        @pl.loop(0, SIDE)
        def _(step):
            at = pl.ds(pl.multiple_of(step * rows, rows), rows)
            q_place = (sublanes((rows, 1)) + (me[0] ^ step) * rows).astype(F32)
            q_place = jnp.concatenate([q_place, q_place], axis=0)
            allowed = (k_place <= q_place) & (k_place >= start_of(q_place, cuts))
            scores = right_dot(two_heads(query[at, here]), k_two[...]) * SCALE
            scores = jnp.where(allowed, scores, MASKED)
            expd = jnp.exp(scores - jnp.max(scores, axis=-1, keepdims=True))
            probs = (expd * (1.0 / jnp.sum(expd, axis=-1, keepdims=True))).astype(BF16)
            both = dot(probs, v_two[...])
            mixed[at, here] = jnp.where(
                lanes((rows, 128)) < HD, both[:rows], both[rows:]
            ).astype(BF16)


def backward_kernel(me, *refs):
    d_mixed, attended = refs[:SIDE], refs[SIDE : 2 * SIDE]
    query, key, value, q_raw, k_raw, cosine, sine, normed = refs[2 * SIDE : 2 * SIDE + 8]
    gains, bounds, d_q_raw, d_kv_raw, keep, send = refs[2 * SIDE + 8 : 2 * SIDE + 14]
    k_two, v_two, d_k, d_v, d_q, d_both, k_place, all_attended, d_cols = refs[2 * SIDE + 14 :]
    rows = d_mixed[0].shape[0]
    length = key.shape[0]
    q_cols = query.shape[1]
    pairs = q_cols // 128
    q_gain, k_gain = gains[2:3, :128], gains[3:4, :128]
    cuts = [bounds[0:1, :], bounds[1:2, :]]
    for part in range(SIDE):
        at = pl.ds(part * rows, rows)
        d_both[at, :] = d_mixed[part][:, :q_cols]
        d_cols[at, :] = d_mixed[part][:, q_cols:]
        all_attended[at, :] = attended[part][...]
    for part in range(length // rows):
        base = (me[0] ^ part) * rows
        k_place[pl.ds(part * rows, rows), :] = (sublanes((rows, 128)) + base).astype(F32)
    for pair in range(pairs):
        here = pl.ds(pair * 128, 128)
        k_two[...] = doubled(key[...], pair)
        v_two[...] = doubled(value[...], pair)
        d_k[pair] = jnp.zeros((length, 128), F32)
        d_v[pair] = jnp.zeros((length, 128), F32)

        @pl.loop(0, SIDE)
        def _(step):
            at = pl.ds(pl.multiple_of(step * rows, rows), rows)
            q_place = (lanes((1, rows)) + (me[0] ^ step) * rows).astype(F32)
            allowed = (k_place[...] <= q_place) & (k_place[...] >= start_of(q_place, cuts))
            allowed = jnp.concatenate([allowed, allowed], axis=1)
            q_two = two_heads(query[at, here])
            d_two = two_heads(d_both[at, here])
            scores = jnp.where(allowed, right_dot(k_two[...], q_two) * SCALE, MASKED)
            expd = jnp.exp(scores - jnp.max(scores, axis=0, keepdims=True))
            probs = expd * (1.0 / jnp.sum(expd, axis=0, keepdims=True))
            d_probs = right_dot(v_two[...], d_two)
            delta = jnp.sum(probs * d_probs, axis=0, keepdims=True)
            d_scores = (probs * (d_probs - delta)).astype(BF16)
            d_v[pair] += dot(probs.astype(BF16), d_two)
            d_k[pair] += dot(d_scores, q_two)
            both = left_dot(d_scores, k_two[...])
            d_q[at, here] = jnp.where(lanes((rows, 128)) < HD, both[:rows], both[rows:]) * SCALE

    first = lanes((rows, 128)) < HD
    sums = [jnp.zeros((1, 128), F32), jnp.zeros((1, 128), F32)]

    def back(incoming, raw, gain, at, which):
        inverse = lax.rsqrt(head_mean(raw * raw) + EPS)
        normal = raw * inverse
        incoming = incoming.astype(BF16).astype(F32)
        turned = incoming * cosine[at, :] - partner(incoming) * sine[at, :]
        sums[which] = sums[which] + jnp.sum(turned * normal, axis=0, keepdims=True)
        turned = turned * gain
        return (inverse * (turned - normal * head_mean(turned * normal))).astype(BF16)

    def joined(pieces):
        pieces = [piece + pltpu.roll(piece, HD, 1) for piece in pieces]
        return jnp.where(first, pieces[0], pieces[1])

    for part in range(length // rows):
        at = pl.ds(part * rows, rows)
        if part < SIDE:
            for pair in range(pairs):
                here = pl.ds(pair * 128, 128)
                d_q_raw[at, here] = back(d_q[at, here], q_raw[at, here], q_gain, at, 0)
        d_key = joined([d_k[pair, at, :] for pair in range(pairs)]) * SCALE
        d_kv_raw[at, :128] = back(d_key, k_raw[at, :], k_gain, at, 1)
        d_kv_raw[at, 128:] = joined([d_v[pair, at, :] for pair in range(pairs)]).astype(BF16)

    half = SIDE * rows
    width = normed.shape[1]
    shard = HD
    few = HD * shard // width
    sums = [total + pltpu.roll(total, HD, 1) for total in sums]
    row, lane = sublanes((8, 128)), lanes((8, 128))

    def gain_block(p):
        there = (row < few) & (lane == p * few + row)
        sides = [jnp.sum(jnp.where(there, total, 0.0), axis=1, keepdims=True) for total in sums]
        block = jnp.where(lane == 0, sides[0], jnp.where(lane == 1, sides[1], 0.0))
        return jnp.concatenate([block, jnp.zeros((shard - 8, 128), F32)], axis=0)

    first_core = me[1] == 0
    for chunk in range(width // 256):
        here = pl.ds(chunk * 256, 256)
        terms = jnp.concatenate(
            [
                left_dot(normed[:half, here], d_q_raw[...]),
                left_dot(normed[:, here], d_kv_raw[...]),
                left_dot(all_attended[:, here], d_cols[...]),
            ],
            axis=1,
        )
        for pair in range(256 // (2 * shard)):
            blocks = []
            for core in range(2):
                begin = (2 * pair + core) * shard
                p = begin // shard + chunk * (256 // shard)
                blocks.append(
                    jnp.concatenate([terms[begin : begin + shard], gain_block(p)], axis=1)
                )
            at = pl.ds((chunk * (256 // shard) // 2 + pair) * shard, shard)
            keep[at, :] = jnp.where(first_core, blocks[0], blocks[1]).astype(BF16)
            send[at, :] = jnp.where(first_core, blocks[1], blocks[0]).astype(BF16)


def terms_kernel(where, tokens, d_gate, d_up, hidden, cot, down, keep, send, out_part, grad_down):
    first_core = where[1] == 0
    shard = HD
    cols = d_gate.shape[1]
    tall = keep.shape[0] // 8
    width = tokens.shape[1]
    piece = hidden.shape[1] // 16
    wide = 2 * cols - 2 * width

    def store(block, begin, here, one, two):
        at = pl.ds(block * tall + begin, one.shape[0])
        keep[at, here] = jnp.where(first_core, one, two).astype(BF16)
        send[at, here] = jnp.where(first_core, two, one).astype(BF16)

    for chunk in range(width // 256):
        left = tokens[:, chunk * 256 : (chunk + 1) * 256]
        for which, right in enumerate((d_gate, d_up)):
            here = pl.ds(which * cols, cols)
            terms = left_dot(left, right[...]).reshape(2, 2, shard, cols)
            for pair in range(2):
                store(chunk * 2 + pair, 0, here, terms[pair, 0], terms[pair, 1])
    for chunk in range(hidden.shape[1] // 384):
        here = pl.ds(chunk * 384, 384)
        grad_down[here, :] = left_dot(hidden[:, here], cot[...])

    def folded(p):
        rows = grad_down[p * piece : (p + 1) * piece, :]
        rest = [rows[64:, j * wide : (j + 1) * wide] for j in range(width // wide)]
        return jnp.concatenate([rows[:32], rows[32:64], jnp.concatenate(rest, axis=0)], axis=1)

    for block in range(8):
        store(block, shard, pl.ds(0, 2 * cols), folded(2 * block), folded(2 * block + 1))
    for chunk in range(hidden.shape[0] // 128):
        at = pl.ds(chunk * 128, 128)
        out_part[at, :] = dot(hidden[at, :], down[...]).astype(BF16)


def pick_kernel(piece, side, gate, up, out):
    for j in range(SIDE):

        @pl.when(side[0] == j)
        def _():
            pieces = []
            for weight in (gate, up):
                values = weight[...].astype(F32)
                for begin in range(j * piece, values.shape[1], SIDE * piece):
                    pieces.append(values[:, begin : begin + piece])
            out[...] = jnp.concatenate(pieces, axis=1).astype(BF16)


def place_kernel(piece, shards_count, *refs):
    side = refs[0]
    big, small = refs[1 : 1 + SIDE], refs[1 + SIDE : 1 + 2 * SIDE]
    weights = refs[1 + 2 * SIDE : 6 + 2 * SIDE]
    outs = refs[6 + 2 * SIDE : -2]
    big_all, small_all = refs[-2:]
    for k in range(SIDE):
        big_all[side[0] ^ k] = big[k][...]
        small_all[side[0] ^ k] = small[k][...]
    out_query, out_key, out_value, out_out, out_gate, out_up, out_down, out_gains = outs
    shard = out_gate.shape[0]
    ff_cols = piece * shards_count
    for j in range(SIDE):
        mine = small_all[j].astype(F32)
        begin = 0
        for out in (out_query, out_key, out_value, out_out):
            count = out.shape[1] // SIDE
            out[:, j * count : (j + 1) * count] = mine[:, begin : begin + count]
            begin += count
        out_gains[...] = mine[:, begin:] if j == 0 else out_gains[...] + mine[:, begin:]
        folded = big_all[j, shard:, :].astype(F32)
        width = out_down.shape[1]
        out_down[j * piece : j * piece + 32, :] = folded[:, :width]
        out_down[j * piece + 32 : j * piece + 64, :] = folded[:, width : 2 * width]
        rest = [folded[8 * i : 8 * i + 8, 2 * width :] for i in range(4)]
        out_down[j * piece + 64 : (j + 1) * piece, :] = jnp.concatenate(rest, axis=1)
    for which, out in enumerate((out_gate, out_up)):
        pieces = []
        both = [
            big_all[j, :shard, which * ff_cols : (which + 1) * ff_cols].astype(F32)
            for j in range(SIDE)
        ]
        for p in range(shards_count):
            for j in range(SIDE):
                pieces.append(both[j][:, p * piece : (p + 1) * piece])
        out[...] = jnp.concatenate(pieces, axis=1)

    def products(pairs):
        return sum(
            jnp.sum(out[...] * weight[...].astype(F32), axis=1, keepdims=True)
            for out, weight in pairs
        )

    attn = products(zip((out_query, out_key, out_value), weights[:3]))
    ffn = products(zip((out_gate, out_up), weights[3:]))
    lane = lanes(out_gains.shape)
    out_gains[...] = jnp.where(lane == 2, attn, jnp.where(lane == 3, ffn, out_gains[...]))


def shards(
    inputs,
    doc_ids,
    w_query,
    w_key,
    w_value,
    w_out,
    w_gate,
    w_up,
    w_down,
    attn_gain,
    ffn_gain,
    query_gain,
    key_gain,
    cotangent,
):
    rows, width = inputs.shape[1:]
    seqs = lax.axis_size("seq")
    dps = lax.axis_size("dp")
    me = lax.axis_index("seq").astype(jnp.uint32)
    side = me & (SIDE - 1)
    length = rows * seqs
    half = rows * SIDE
    shard = w_query.shape[0]
    q_cols = H * HD // SIDE
    kv_cols = KV * HD // SIDE
    ff = w_gate.shape[1]
    ff_cols = ff // SIDE
    piece = w_down.shape[0] // SIDE
    tall = max(piece, shard)
    cols = q_cols + 2 * kv_cols

    def columns(weight, count):
        return lax.dynamic_slice_in_dim(weight, side * count, count, axis=1)

    def out(*shape, dtype=F32):
        return jax.ShapeDtypeStruct(shape, dtype)

    params = pltpu.CompilerParams(vmem_limit_bytes=VMEM_LIMIT)

    tokens = inputs[0]
    cot = cotangent[0]
    mine = lax.axis_index("dp").astype(jnp.uint32)
    core, x, z = mine & 1, (mine >> 1) & 1, mine >> 2
    few = HD // dps
    smem = pl.BlockSpec(memory_space=pltpu.SMEM)
    me_ref = me.astype(jnp.int32).reshape(1)
    attn_pack = pl.pallas_call(
        functools.partial(pack_kernel, few),
        out_shape=out(shard + 16, cols + width, dtype=BF16),
        in_specs=[smem] + [pl.BlockSpec(memory_space=pltpu.HBM)] * 4 + whole(1),
        out_specs=pl.BlockSpec(memory_space=pl.ANY),
        scratch_shapes=[pltpu.VMEM((16, cols + width), BF16), pltpu.SemaphoreType.DMA((5,))],
    )(
        jnp.stack([side, mine]).astype(jnp.int32),
        w_query,
        w_key,
        w_value,
        w_out,
        jnp.concatenate([attn_gain, ffn_gain, query_gain, key_gain])[None],
    )
    attn_all = lax.all_gather(attn_pack, "dp", axis=0, tiled=False)
    ids = jnp.pad(doc_ids.astype(BF16), ((0, 15), (0, width - rows)))
    message = jnp.concatenate([tokens, ids], axis=0)
    token_parts = [message] + [swap(message, "seq", k) for k in range(1, SIDE)]
    earlier = lax.ppermute(message, "seq", [(i, i ^ SIDE) for i in range(SIDE)])
    token_parts.append(earlier)
    for k in range(1, SIDE):
        token_parts.append(lax.ppermute(earlier, "seq", [(i, i ^ k) for i in range(SIDE, seqs)]))
    cot_parts = gather_side(cot)

    side_ref = side.astype(jnp.int32).reshape(1)
    picked = pl.pallas_call(
        functools.partial(pick_kernel, piece),
        out_shape=out(shard, 2 * ff_cols, dtype=BF16),
        in_specs=[smem] + whole(2),
        out_specs=whole(1)[0],
        compiler_params=params,
    )(side_ref, w_gate, w_up)
    down_piece = lax.dynamic_slice_in_dim(w_down, side * piece, piece, axis=0)
    pack = jnp.concatenate(
        [
            jnp.pad(picked, ((0, tall - shard), (0, 0))),
            jnp.pad(down_piece, ((0, tall - piece), (0, 0))),
        ],
        axis=1,
    )
    packed = lax.all_gather(pack, "dp", axis=0, tiled=False)
    w_qkv = attn_all[:, :shard, :cols].reshape(width, cols)
    wo = attn_all[:, :shard, cols:].reshape(H * HD, width)
    w_gate_up = packed[:, :shard, : 2 * ff_cols].reshape(width, 2 * ff_cols)
    wd = packed[:, :piece, 2 * ff_cols :].reshape(ff_cols, width)

    freqs = BASE ** (-(jnp.arange(HD // 2, dtype=F32) * (2.0 / HD)))
    freqs = jnp.concatenate([freqs] * 4)
    angles = jnp.arange(length, dtype=jnp.int32).astype(F32)[:, None] * freqs[None, :]

    normed, q_raw, k_raw, query, key, value, mixed, gains, cosine, sine, bounds = pl.pallas_call(
        functools.partial(forward_kernel, seqs),
        out_shape=(
            out(length, width, dtype=BF16),
            out(half, q_cols),
            out(length, kv_cols),
            out(half, q_cols, dtype=BF16),
            out(length, kv_cols, dtype=BF16),
            out(length, kv_cols, dtype=BF16),
            out(half, q_cols, dtype=BF16),
            out(16, width),
            out(length, 128),
            out(length, 128),
            out(8, 128),
        ),
        in_specs=[smem] + whole(seqs + 3),
        out_specs=tuple(whole(11)),
        scratch_shapes=[pltpu.VMEM((length, 128), BF16)] * 2,
        compiler_params=params,
        cost_estimate=pl.CostEstimate(
            flops=10_000_000_000, bytes_accessed=10_000_000, transcendentals=2_000_000
        ),
    )(me_ref, *token_parts, attn_all, jnp.cos(angles), jnp.sin(angles))
    attn_g = gains[0:1]
    ffn_g = gains[1:2]

    mixed = tie(mixed, *cot_parts)
    mixed_parts = scatter_side([mixed[k * rows : (k + 1) * rows] for k in range(SIDE)])
    attended_parts = jnp.stack(mixed_parts)
    attended = jnp.concatenate(
        [
            lax.dynamic_index_in_dim(attended_parts, side ^ j, axis=0, keepdims=False)
            for j in range(SIDE)
        ],
        axis=1,
    )
    states = tokens.astype(F32)
    resid = states + dot(attended, wo)
    normal2, inverse2 = norm_parts(resid)
    normed2 = (normal2 * ffn_g).astype(BF16)

    normed2_all = jnp.concatenate(gather_side(tie(normed2, w_qkv)), axis=0)
    attended_parts = gather_side(tie(attended, normed2_all))
    cot_all = jnp.concatenate(cot_parts, axis=0)
    gate_up = dot(normed2_all, w_gate_up)
    gate, upper = gate_up[:, :ff_cols], gate_up[:, ff_cols:]
    d_hidden = right_dot(cot_all, wd)
    sigmoid_gate = jax.nn.sigmoid(gate)
    active = gate * sigmoid_gate
    hidden = (active * upper).astype(BF16)
    d_gate = d_hidden * upper * sigmoid_gate * (1.0 + gate * (1.0 - sigmoid_gate))
    d_upper = d_hidden * active
    d_gate, d_upper = d_gate.astype(BF16), d_upper.astype(BF16)
    d_gate_up = jnp.concatenate([d_gate, d_upper], axis=1)
    d_normed2_part = right_dot(d_gate_up, w_gate_up).astype(BF16)

    def scatter_rows(blocks):
        return scatter_side([blocks[k * rows : (k + 1) * rows] for k in range(SIDE)])

    def sum_parts(received):
        return sum(part.astype(F32) for part in received)

    d_normed2_parts = scatter_rows(d_normed2_part)

    where = jnp.stack([me, core]).astype(jnp.int32)
    gate_up_keep, gate_up_send, down_part = pl.pallas_call(
        terms_kernel,
        out_shape=(
            out(dps // 2 * (shard + 32), 2 * ff_cols, dtype=BF16),
            out(dps // 2 * (shard + 32), 2 * ff_cols, dtype=BF16),
            out(half, width, dtype=BF16),
        ),
        in_specs=[smem] + whole(6),
        out_specs=tuple(whole(3)),
        scratch_shapes=[pltpu.VMEM((ff_cols, width), F32)],
        compiler_params=params,
        cost_estimate=pl.CostEstimate(
            flops=10_000_000_000, bytes_accessed=20_000_000, transcendentals=0
        ),
    )(
        where,
        normed2_all,
        tie(d_gate, d_normed2_part, *attended_parts),
        d_upper,
        hidden,
        cot_all,
        wd,
    )
    d_normed2_parts[0] = tie(d_normed2_parts[0], down_part)
    d_normed2 = sum_parts(d_normed2_parts)
    gate_up_got = swap(tie(gate_up_send, d_normed2), "dp", 1)

    d_resid = cot.astype(F32) + norm_back(d_normed2 * ffn_g, normal2, inverse2)
    d_resid_low = d_resid.astype(BF16)
    d_attended = right_dot(d_resid_low, wo).astype(BF16)
    out_cols = width // SIDE
    d_messages = scatter_side(
        [
            jnp.concatenate(
                [
                    lax.dynamic_slice_in_dim(d_attended, (side ^ k) * q_cols, q_cols, axis=1),
                    lax.dynamic_slice_in_dim(d_resid_low, (side ^ k) * out_cols, out_cols, axis=1),
                ],
                axis=1,
            )
            for k in range(SIDE)
        ]
    )
    gate_up_sum = added(gate_up_keep, tie(gate_up_got, d_attended))
    gate_up_parts = send_along_z(gate_up_sum.reshape(4, 2, shard + 32, -1), mine)
    down_parts = scatter_rows(tie(down_part, *d_messages))

    d_q_raw, d_kv_raw, attn_keep, attn_send = pl.pallas_call(
        backward_kernel,
        out_shape=(
            out(half, q_cols, dtype=BF16),
            out(length, 2 * kv_cols, dtype=BF16),
            out(width // 2, cols + out_cols + 128, dtype=BF16),
            out(width // 2, cols + out_cols + 128, dtype=BF16),
        ),
        in_specs=[smem] + whole(2 * SIDE + 10),
        out_specs=tuple(whole(4)),
        scratch_shapes=[
            pltpu.VMEM((length, 128), BF16),
            pltpu.VMEM((length, 128), BF16),
            pltpu.VMEM((2, length, 128), F32),
            pltpu.VMEM((2, length, 128), F32),
            pltpu.VMEM((half, q_cols), F32),
            pltpu.VMEM((half, q_cols), BF16),
            pltpu.VMEM((length, 128), F32),
            pltpu.VMEM((half, width), BF16),
            pltpu.VMEM((half, out_cols), BF16),
        ],
        compiler_params=params,
        cost_estimate=pl.CostEstimate(
            flops=14_000_000_000, bytes_accessed=10_000_000, transcendentals=2_000_000
        ),
    )(
        where,
        *d_messages,
        *attended_parts,
        query,
        key,
        value,
        q_raw,
        k_raw,
        cosine,
        sine,
        normed,
        gains,
        bounds,
    )
    gate_up_parts[0] = tie(gate_up_parts[0], d_kv_raw)
    gate_up_sum = added(*gate_up_parts)
    gate_up_got = swap(take(gate_up_sum, 1 - x, 0), "dp", 2)
    attn_got = swap(attn_send, "dp", 1)
    from_later = lax.ppermute(
        d_kv_raw[half:], "seq", [(i, i - SIDE) for i in range(SIDE, seqs)]
    )
    attn_sum = added(attn_keep, tie(attn_got, gate_up_sum))
    attn_parts = send_along_z(attn_sum.reshape(4, 2, shard, -1), mine)
    d_kv = added(d_kv_raw[:half], tie(from_later, attn_sum))
    d_qkv = jnp.concatenate([d_q_raw, d_kv], axis=1)
    d_normed_part = right_dot(d_qkv, w_qkv).astype(BF16)
    d_normed_parts = scatter_rows(d_normed_part)
    gate_up_share = added(take(gate_up_sum, x, 0), tie(gate_up_got, d_normed_part))
    gate_up_other = swap(gate_up_share, "seq", SIDE)
    attn_parts[0] = tie(attn_parts[0], gate_up_share)
    attn_sum = added(*attn_parts)
    attn_got = swap(take(attn_sum, 1 - x, 0), "dp", 2)
    down_parts[0] = tie(down_parts[0], attn_sum)
    block_out = (resid + sum_parts(down_parts)).astype(BF16)
    attn_share = added(take(attn_sum, x, 0), tie(attn_got, block_out))
    attn_other = swap(attn_share, "seq", SIDE)
    gate_up_share = added(gate_up_share, tie(gate_up_other, attn_share))
    gate_up_parts = gather_side(gate_up_share)
    attn_share = added(attn_share, tie(attn_other, gate_up_share))
    attn_parts = gather_side(attn_share)
    d_normed_parts[0] = tie(d_normed_parts[0], attn_share)
    d_normed = sum_parts(d_normed_parts)
    normal1, inverse1 = norm_parts(states)
    grad_inputs = d_resid + norm_back(d_normed * attn_g, normal1, inverse1)

    outs = pl.pallas_call(
        functools.partial(place_kernel, piece, dps),
        out_shape=(
            out(shard, H * HD),
            out(shard, KV * HD),
            out(shard, KV * HD),
            out(shard, width),
            out(shard, ff),
            out(shard, ff),
            out(SIDE * piece, width),
            out(shard, 128),
        ),
        in_specs=[smem] + whole(2 * SIDE + 5),
        out_specs=tuple(whole(8)),
        scratch_shapes=[
            pltpu.VMEM((SIDE,) + gate_up_share.shape, BF16),
            pltpu.VMEM((SIDE,) + attn_share.shape, BF16),
        ],
        compiler_params=params,
    )(
        side_ref,
        *gate_up_parts,
        *attn_parts,
        w_query,
        w_key,
        w_value,
        w_gate,
        w_up,
    )
    out_query, out_key, out_value, out_out, out_gate, out_up, out_down, out_gains = outs
    return (
        block_out[None],
        grad_inputs[None],
        out_query,
        out_key,
        out_value,
        out_out,
        out_gate,
        out_up,
        out_down,
        out_gains[:, 2] / attn_gain.astype(F32),
        out_gains[:, 3] / ffn_gain.astype(F32),
        out_gains[:few, 0],
        out_gains[:few, 1],
    )


def solution(mesh):
    tokens = P("dp", "seq", None)
    weight = P("dp", None)
    gain = P("dp")
    return jax.shard_map(
        shards,
        mesh=mesh,
        in_specs=(tokens, P("dp", "seq")) + (weight,) * 7 + (gain,) * 4 + (tokens,),
        out_specs=(tokens, tokens) + (weight,) * 7 + (gain,) * 4,
        check_vma=False,
    )
```

```python
import functools

import jax
import jax.numpy as jnp
from jax import lax
from jax.experimental import pallas as pl
from jax.experimental.pallas import tpu as pltpu
from jax.sharding import PartitionSpec as P

H = 16
KV = 8
HD = 64
SIDE = 4

EPS = 1e-05
BASE = 1000000.0
MASKED = -1e30
SCALE = HD ** (-0.5)
BF16 = jnp.bfloat16
F32 = jnp.float32
VMEM_LIMIT = 50 * 1024 * 1024


def left_dot(left, right):
    return lax.dot_general(left, right, (((0,), (0,)), ((), ())), preferred_element_type=F32)


def right_dot(left, right):
    return lax.dot_general(left, right, (((1,), (1,)), ((), ())), preferred_element_type=F32)


def dot(left, right):
    return lax.dot_general(left, right, (((1,), (0,)), ((), ())), preferred_element_type=F32)


def norm_parts(values):
    inverse = lax.rsqrt(jnp.mean(values * values, axis=-1, keepdims=True) + EPS)
    return (values * inverse, inverse)


def norm_back(incoming, normal, inverse):
    return inverse * (incoming - normal * jnp.mean(incoming * normal, axis=-1, keepdims=True))


def swap(block, axis, step):
    size = lax.axis_size(axis)
    return lax.ppermute(block, axis, [(i, i ^ step) for i in range(size)])


def gather_side(block):
    return [block] + [swap(block, "seq", k) for k in range(1, SIDE)]


def scatter_side(blocks):
    return [blocks[0]] + [swap(blocks[k], "seq", k) for k in range(1, SIDE)]


def tie(value, *after):
    return lax.optimization_barrier((value,) + after)[0]


def take(array, index, axis):
    return lax.dynamic_index_in_dim(array, index, axis=axis, keepdims=False)


def added(*pieces):
    return sum(piece.astype(F32) for piece in pieces).astype(BF16)


def send_along_z(total, mine):
    z = mine >> 2
    return [take(total, z, 0)] + [swap(take(total, z ^ k, 0), "dp", 4 * k) for k in range(1, 4)]


def whole(count):
    return [pl.BlockSpec(memory_space=pltpu.VMEM)] * count


def lanes(shape):
    return lax.broadcasted_iota(jnp.int32, shape, len(shape) - 1)


def head_mean(values):
    row = lax.broadcasted_iota(jnp.int32, (128, 128), 0)
    ones = jnp.where(row // HD == lanes((128, 128)) // HD, 1.0 / HD, 0.0).astype(BF16)
    high = values.astype(BF16)
    rest = (values - high.astype(F32)).astype(BF16)
    return dot(high, ones) + dot(rest, ones)


def partner(values):
    return jnp.where(
        lanes(values.shape) % HD < HD // 2,
        pltpu.roll(values, 128 - HD // 2, 1),
        pltpu.roll(values, HD // 2, 1),
    )


def doubled(pair, head):
    other = pltpu.roll(pair.astype(F32), HD, 1).astype(pair.dtype)
    first = lanes(pair.shape) < HD
    return jnp.where(first, pair, other) if head == 0 else jnp.where(first, other, pair)


def two_heads(block):
    first = lanes(block.shape) < HD
    zero = jnp.zeros_like(block)
    return jnp.concatenate([jnp.where(first, block, zero), jnp.where(first, zero, block)], axis=0)


def sublanes(shape):
    return lax.broadcasted_iota(jnp.int32, shape, len(shape) - 2)


def pack_kernel(few, where, query, key, value, out_weight, gains, pack, scratch, sems):
    side, mine = where[0], where[1]
    shard, width = out_weight.shape
    copies = []
    begin = 0
    for weight in (query, key, value):
        count = weight.shape[1] // SIDE
        at = pl.ds(pl.multiple_of(side * count, count), count)
        copies.append((weight.at[:, at], pack.at[pl.ds(0, shard), pl.ds(begin, count)]))
        begin += count
    copies.append((out_weight, pack.at[pl.ds(0, shard), pl.ds(begin, width)]))
    copies = [
        pltpu.make_async_copy(source, target, sems.at[index])
        for index, (source, target) in enumerate(copies)
    ]
    for copy in copies:
        copy.start()

    def spread(gain, count, lane_count):
        row = jnp.concatenate([gain] * (lane_count // count), axis=1)
        return row, lanes(row.shape)

    all_gains = gains[...].astype(F32)
    rows = []
    for gain in (all_gains[:, :shard], all_gains[:, shard : 2 * shard]):
        row, lane = spread(gain, shard, width)
        rows.append(jnp.where(lane // shard == mine, row, 0.0))
    for index in range(2):
        gain = all_gains[:, 2 * shard + index * few : 2 * shard + (index + 1) * few]
        row, lane = spread(gain, few, 128)
        row = jnp.where(lane % HD // few == mine, row, 0.0)
        rows.append(jnp.concatenate([row, jnp.zeros((1, width - 128), F32)], axis=1))
    at = sublanes((16, width))
    extra = jnp.zeros((16, width), F32)
    for index, row in enumerate(rows):
        extra = jnp.where(at == index, row, extra)
    extra = jnp.concatenate([extra, jnp.zeros((16, begin), F32)], axis=1)
    scratch[...] = extra.astype(BF16)
    last = pltpu.make_async_copy(scratch, pack.at[pl.ds(shard, 16), :], sems.at[len(copies)])
    last.start()
    for copy in copies + [last]:
        copy.wait()


def start_of(place, cuts):
    return jnp.where(place >= cuts[1], cuts[1], jnp.where(place >= cuts[0], cuts[0], 0.0))


def forward_kernel(parts, me, *refs):
    token_refs = refs[:parts]
    packed, cos_table, sin_table = refs[parts : parts + 3]
    normed_out, q_raw, k_raw, query, key, value, mixed, gains = refs[parts + 3 : parts + 11]
    cosine, sine, bounds, k_two, v_two = refs[parts + 11 :]
    rows = query.shape[0] // SIDE
    width = token_refs[0].shape[1]
    q_cols = query.shape[1]
    cols = q_cols + 2 * key.shape[1]
    shard = packed.shape[1] - 16
    weight = packed[:, :shard, :cols].reshape(width, cols)
    gains[...] = jnp.sum(packed[:, shard:, :width].astype(F32), axis=0)
    gain, q_gain, k_gain = gains[0:1, :], gains[2:3, :128], gains[3:4, :128]

    bases = [(me[0] ^ part) * rows for part in range(parts)]
    row_places = [(lanes((1, rows)) + base).astype(F32) for base in bases]
    cuts = []
    for number in (1.0, 2.0):
        least = jnp.full((1, rows), 4096.0, F32)
        for part in range(parts):
            ids = token_refs[part][rows:, :rows].astype(F32)[0:1]
            least = jnp.minimum(least, jnp.where(ids == number, row_places[part], 4096.0))
        cuts.append(jnp.min(least, axis=1, keepdims=True))
    for index in range(2):
        bounds[index : index + 1, :] = jnp.broadcast_to(cuts[index], (1, 128))
    at_cut = []
    all_places = sublanes(cos_table.shape).astype(F32)
    for cut in cuts:
        there = all_places == cut
        at_cut.append(
            [
                jnp.sum(jnp.where(there, table[...], 0.0), axis=0, keepdims=True)
                for table in (cos_table, sin_table)
            ]
        )
    sign = jnp.where(lanes((1, 128)) % HD < HD // 2, -1.0, 1.0)

    for part in range(parts):
        at = pl.ds(part * rows, rows)
        states = token_refs[part][:rows, :].astype(F32)
        inverse = lax.rsqrt(jnp.mean(states * states, axis=-1, keepdims=True) + EPS)
        normed = (states * inverse * gain).astype(BF16)
        there = pl.ds(pl.multiple_of(bases[part], rows), rows)
        place = (sublanes((rows, 128)) + bases[part]).astype(F32)
        cos_cut = jnp.where(
            place >= cuts[1], at_cut[1][0], jnp.where(place >= cuts[0], at_cut[0][0], 1.0)
        )
        sin_cut = jnp.where(
            place >= cuts[1], at_cut[1][1], jnp.where(place >= cuts[0], at_cut[0][1], 0.0)
        )
        cos = cos_table[there, :] * cos_cut + sin_table[there, :] * sin_cut
        sin = (sin_table[there, :] * cos_cut - cos_table[there, :] * sin_cut) * sign
        cosine[at, :] = cos
        sine[at, :] = sin
        normed_out[at, :] = normed
        if part < SIDE:
            raw = dot(normed, weight)
            raw_q, raw_kv = raw[:, :q_cols], raw[:, q_cols:]
            q_raw[at, :] = raw_q
            for pair in range(q_cols // 128):
                here = pl.ds(pair * 128, 128)
                one = raw_q[:, pair * 128 : (pair + 1) * 128]
                scaled = one * lax.rsqrt(head_mean(one * one) + EPS) * q_gain
                query[at, here] = (scaled * cos + partner(scaled) * sin).astype(BF16)
        else:
            raw_kv = dot(normed, weight[:, q_cols:])
        one = raw_kv[:, :128]
        k_raw[at, :] = one
        scaled = one * lax.rsqrt(head_mean(one * one) + EPS) * k_gain
        key[at, :] = (scaled * cos + partner(scaled) * sin).astype(BF16)
        value[at, :] = raw_kv[:, 128:].astype(BF16)
    k_place = jnp.concatenate(row_places, axis=1)
    for pair in range(q_cols // 128):
        here = pl.ds(pair * 128, 128)
        k_two[...] = doubled(key[...], pair)
        v_two[...] = doubled(value[...], pair)

        @pl.loop(0, SIDE)
        def _(step):
            at = pl.ds(pl.multiple_of(step * rows, rows), rows)
            q_place = (sublanes((rows, 1)) + (me[0] ^ step) * rows).astype(F32)
            q_place = jnp.concatenate([q_place, q_place], axis=0)
            allowed = (k_place <= q_place) & (k_place >= start_of(q_place, cuts))
            scores = right_dot(two_heads(query[at, here]), k_two[...]) * SCALE
            scores = jnp.where(allowed, scores, MASKED)
            expd = jnp.exp(scores - jnp.max(scores, axis=-1, keepdims=True))
            probs = (expd * (1.0 / jnp.sum(expd, axis=-1, keepdims=True))).astype(BF16)
            both = dot(probs, v_two[...])
            mixed[at, here] = jnp.where(
                lanes((rows, 128)) < HD, both[:rows], both[rows:]
            ).astype(BF16)


def backward_kernel(me, *refs):
    d_mixed, attended = refs[:SIDE], refs[SIDE : 2 * SIDE]
    query, key, value, q_raw, k_raw, cosine, sine, normed = refs[2 * SIDE : 2 * SIDE + 8]
    gains, bounds, d_q_raw, d_kv_raw, keep, send = refs[2 * SIDE + 8 : 2 * SIDE + 14]
    k_two, v_two, d_k, d_v, d_q, d_both, k_place, all_attended, d_cols = refs[2 * SIDE + 14 :]
    rows = d_mixed[0].shape[0]
    length = key.shape[0]
    q_cols = query.shape[1]
    pairs = q_cols // 128
    q_gain, k_gain = gains[2:3, :128], gains[3:4, :128]
    cuts = [bounds[0:1, :], bounds[1:2, :]]
    for part in range(SIDE):
        at = pl.ds(part * rows, rows)
        d_both[at, :] = d_mixed[part][:, :q_cols]
        d_cols[at, :] = d_mixed[part][:, q_cols:]
        all_attended[at, :] = attended[part][...]
    for part in range(length // rows):
        base = (me[0] ^ part) * rows
        k_place[pl.ds(part * rows, rows), :] = (sublanes((rows, 128)) + base).astype(F32)
    for pair in range(pairs):
        here = pl.ds(pair * 128, 128)
        k_two[...] = doubled(key[...], pair)
        v_two[...] = doubled(value[...], pair)
        d_k[pair] = jnp.zeros((length, 128), F32)
        d_v[pair] = jnp.zeros((length, 128), F32)

        @pl.loop(0, SIDE)
        def _(step):
            at = pl.ds(pl.multiple_of(step * rows, rows), rows)
            q_place = (lanes((1, rows)) + (me[0] ^ step) * rows).astype(F32)
            allowed = (k_place[...] <= q_place) & (k_place[...] >= start_of(q_place, cuts))
            allowed = jnp.concatenate([allowed, allowed], axis=1)
            q_two = two_heads(query[at, here])
            d_two = two_heads(d_both[at, here])
            scores = jnp.where(allowed, right_dot(k_two[...], q_two) * SCALE, MASKED)
            expd = jnp.exp(scores - jnp.max(scores, axis=0, keepdims=True))
            probs = expd * (1.0 / jnp.sum(expd, axis=0, keepdims=True))
            d_probs = right_dot(v_two[...], d_two)
            delta = jnp.sum(probs * d_probs, axis=0, keepdims=True)
            d_scores = (probs * (d_probs - delta)).astype(BF16)
            d_v[pair] += dot(probs.astype(BF16), d_two)
            d_k[pair] += dot(d_scores, q_two)
            both = left_dot(d_scores, k_two[...])
            d_q[at, here] = jnp.where(lanes((rows, 128)) < HD, both[:rows], both[rows:]) * SCALE

    first = lanes((rows, 128)) < HD
    sums = [jnp.zeros((1, 128), F32), jnp.zeros((1, 128), F32)]

    def back(incoming, raw, gain, at, which):
        inverse = lax.rsqrt(head_mean(raw * raw) + EPS)
        normal = raw * inverse
        incoming = incoming.astype(BF16).astype(F32)
        turned = incoming * cosine[at, :] - partner(incoming) * sine[at, :]
        sums[which] = sums[which] + jnp.sum(turned * normal, axis=0, keepdims=True)
        turned = turned * gain
        return (inverse * (turned - normal * head_mean(turned * normal))).astype(BF16)

    def joined(pieces):
        pieces = [piece + pltpu.roll(piece, HD, 1) for piece in pieces]
        return jnp.where(first, pieces[0], pieces[1])

    for part in range(length // rows):
        at = pl.ds(part * rows, rows)
        if part < SIDE:
            for pair in range(pairs):
                here = pl.ds(pair * 128, 128)
                d_q_raw[at, here] = back(d_q[at, here], q_raw[at, here], q_gain, at, 0)
        d_key = joined([d_k[pair, at, :] for pair in range(pairs)]) * SCALE
        d_kv_raw[at, :128] = back(d_key, k_raw[at, :], k_gain, at, 1)
        d_kv_raw[at, 128:] = joined([d_v[pair, at, :] for pair in range(pairs)]).astype(BF16)

    half = SIDE * rows
    width = normed.shape[1]
    shard = HD
    few = HD * shard // width
    sums = [total + pltpu.roll(total, HD, 1) for total in sums]
    row, lane = sublanes((8, 128)), lanes((8, 128))

    def gain_block(p):
        there = (row < few) & (lane == p * few + row)
        sides = [jnp.sum(jnp.where(there, total, 0.0), axis=1, keepdims=True) for total in sums]
        block = jnp.where(lane == 0, sides[0], jnp.where(lane == 1, sides[1], 0.0))
        return jnp.concatenate([block, jnp.zeros((shard - 8, 128), F32)], axis=0)

    first_core = me[1] == 0
    for chunk in range(width // 256):
        here = pl.ds(chunk * 256, 256)
        terms = jnp.concatenate(
            [
                left_dot(normed[:half, here], d_q_raw[...]),
                left_dot(normed[:, here], d_kv_raw[...]),
                left_dot(all_attended[:, here], d_cols[...]),
            ],
            axis=1,
        )
        for pair in range(256 // (2 * shard)):
            blocks = []
            for core in range(2):
                begin = (2 * pair + core) * shard
                p = begin // shard + chunk * (256 // shard)
                blocks.append(
                    jnp.concatenate([terms[begin : begin + shard], gain_block(p)], axis=1)
                )
            at = pl.ds((chunk * (256 // shard) // 2 + pair) * shard, shard)
            keep[at, :] = jnp.where(first_core, blocks[0], blocks[1]).astype(BF16)
            send[at, :] = jnp.where(first_core, blocks[1], blocks[0]).astype(BF16)


def terms_kernel(where, tokens, d_gate, d_up, hidden, cot, down, keep, send, out_part, grad_down):
    first_core = where[1] == 0
    shard = HD
    cols = d_gate.shape[1]
    tall = keep.shape[0] // 8
    width = tokens.shape[1]
    piece = hidden.shape[1] // 16
    wide = 2 * cols - 2 * width

    def store(block, begin, here, one, two):
        at = pl.ds(block * tall + begin, one.shape[0])
        keep[at, here] = jnp.where(first_core, one, two).astype(BF16)
        send[at, here] = jnp.where(first_core, two, one).astype(BF16)

    for chunk in range(width // 256):
        left = tokens[:, chunk * 256 : (chunk + 1) * 256]
        for which, right in enumerate((d_gate, d_up)):
            here = pl.ds(which * cols, cols)
            terms = left_dot(left, right[...]).reshape(2, 2, shard, cols)
            for pair in range(2):
                store(chunk * 2 + pair, 0, here, terms[pair, 0], terms[pair, 1])
    for chunk in range(hidden.shape[1] // 384):
        here = pl.ds(chunk * 384, 384)
        grad_down[here, :] = left_dot(hidden[:, here], cot[...])

    def folded(p):
        rows = grad_down[p * piece : (p + 1) * piece, :]
        rest = [rows[64:, j * wide : (j + 1) * wide] for j in range(width // wide)]
        return jnp.concatenate([rows[:32], rows[32:64], jnp.concatenate(rest, axis=0)], axis=1)

    for block in range(8):
        store(block, shard, pl.ds(0, 2 * cols), folded(2 * block), folded(2 * block + 1))
    for chunk in range(hidden.shape[0] // 128):
        at = pl.ds(chunk * 128, 128)
        out_part[at, :] = dot(hidden[at, :], down[...]).astype(BF16)


def pick_kernel(piece, side, gate, up, out):
    for j in range(SIDE):

        @pl.when(side[0] == j)
        def _():
            pieces = []
            for weight in (gate, up):
                values = weight[...].astype(F32)
                for begin in range(j * piece, values.shape[1], SIDE * piece):
                    pieces.append(values[:, begin : begin + piece])
            out[...] = jnp.concatenate(pieces, axis=1).astype(BF16)


def place_kernel(piece, shards_count, *refs):
    side = refs[0]
    big, small = refs[1 : 1 + SIDE], refs[1 + SIDE : 1 + 2 * SIDE]
    weights = refs[1 + 2 * SIDE : 6 + 2 * SIDE]
    outs = refs[6 + 2 * SIDE : -2]
    big_all, small_all = refs[-2:]
    for k in range(SIDE):
        big_all[side[0] ^ k] = big[k][...]
        small_all[side[0] ^ k] = small[k][...]
    out_query, out_key, out_value, out_out, out_gate, out_up, out_down, out_gains = outs
    shard = out_gate.shape[0]
    ff_cols = piece * shards_count
    for j in range(SIDE):
        mine = small_all[j].astype(F32)
        begin = 0
        for out in (out_query, out_key, out_value, out_out):
            count = out.shape[1] // SIDE
            out[:, j * count : (j + 1) * count] = mine[:, begin : begin + count]
            begin += count
        out_gains[...] = mine[:, begin:] if j == 0 else out_gains[...] + mine[:, begin:]
        folded = big_all[j, shard:, :].astype(F32)
        width = out_down.shape[1]
        out_down[j * piece : j * piece + 32, :] = folded[:, :width]
        out_down[j * piece + 32 : j * piece + 64, :] = folded[:, width : 2 * width]
        rest = [folded[8 * i : 8 * i + 8, 2 * width :] for i in range(4)]
        out_down[j * piece + 64 : (j + 1) * piece, :] = jnp.concatenate(rest, axis=1)
    for which, out in enumerate((out_gate, out_up)):
        pieces = []
        both = [
            big_all[j, :shard, which * ff_cols : (which + 1) * ff_cols].astype(F32)
            for j in range(SIDE)
        ]
        for p in range(shards_count):
            for j in range(SIDE):
                pieces.append(both[j][:, p * piece : (p + 1) * piece])
        out[...] = jnp.concatenate(pieces, axis=1)

    def products(pairs):
        return sum(
            jnp.sum(out[...] * weight[...].astype(F32), axis=1, keepdims=True)
            for out, weight in pairs
        )

    attn = products(zip((out_query, out_key, out_value), weights[:3]))
    ffn = products(zip((out_gate, out_up), weights[3:]))
    lane = lanes(out_gains.shape)
    out_gains[...] = jnp.where(lane == 2, attn, jnp.where(lane == 3, ffn, out_gains[...]))


def shards(
    inputs,
    doc_ids,
    w_query,
    w_key,
    w_value,
    w_out,
    w_gate,
    w_up,
    w_down,
    attn_gain,
    ffn_gain,
    query_gain,
    key_gain,
    cotangent,
):
    rows, width = inputs.shape[1:]
    seqs = lax.axis_size("seq")
    dps = lax.axis_size("dp")
    me = lax.axis_index("seq").astype(jnp.uint32)
    side = me & (SIDE - 1)
    length = rows * seqs
    half = rows * SIDE
    shard = w_query.shape[0]
    q_cols = H * HD // SIDE
    kv_cols = KV * HD // SIDE
    ff = w_gate.shape[1]
    ff_cols = ff // SIDE
    piece = w_down.shape[0] // SIDE
    tall = max(piece, shard)
    cols = q_cols + 2 * kv_cols

    def columns(weight, count):
        return lax.dynamic_slice_in_dim(weight, side * count, count, axis=1)

    def out(*shape, dtype=F32):
        return jax.ShapeDtypeStruct(shape, dtype)

    params = pltpu.CompilerParams(vmem_limit_bytes=VMEM_LIMIT)

    tokens = inputs[0]
    cot = cotangent[0]
    mine = lax.axis_index("dp").astype(jnp.uint32)
    core, x, z = mine & 1, (mine >> 1) & 1, mine >> 2
    few = HD // dps
    smem = pl.BlockSpec(memory_space=pltpu.SMEM)
    me_ref = me.astype(jnp.int32).reshape(1)
    attn_pack = pl.pallas_call(
        functools.partial(pack_kernel, few),
        out_shape=out(shard + 16, cols + width, dtype=BF16),
        in_specs=[smem] + [pl.BlockSpec(memory_space=pl.ANY)] * 4 + whole(1),
        out_specs=pl.BlockSpec(memory_space=pl.ANY),
        scratch_shapes=[pltpu.VMEM((16, cols + width), BF16), pltpu.SemaphoreType.DMA((5,))],
        compiler_params=params,
    )(
        jnp.stack([side, mine]).astype(jnp.int32),
        w_query,
        w_key,
        w_value,
        w_out,
        jnp.concatenate([attn_gain, ffn_gain, query_gain, key_gain])[None],
    )
    attn_all = lax.all_gather(attn_pack, "dp", axis=0, tiled=False)
    ids = jnp.pad(doc_ids.astype(BF16), ((0, 15), (0, width - rows)))
    message = jnp.concatenate([tokens, ids], axis=0)
    token_parts = [message] + [swap(message, "seq", k) for k in range(1, SIDE)]
    earlier = lax.ppermute(message, "seq", [(i, i ^ SIDE) for i in range(SIDE)])
    token_parts.append(earlier)
    for k in range(1, SIDE):
        token_parts.append(lax.ppermute(earlier, "seq", [(i, i ^ k) for i in range(SIDE, seqs)]))
    cot_parts = gather_side(cot)

    side_ref = side.astype(jnp.int32).reshape(1)
    picked = pl.pallas_call(
        functools.partial(pick_kernel, piece),
        out_shape=out(shard, 2 * ff_cols, dtype=BF16),
        in_specs=[smem] + whole(2),
        out_specs=whole(1)[0],
        compiler_params=params,
    )(side_ref, w_gate, w_up)
    down_piece = lax.dynamic_slice_in_dim(w_down, side * piece, piece, axis=0)
    pack = jnp.concatenate(
        [
            jnp.pad(picked, ((0, tall - shard), (0, 0))),
            jnp.pad(down_piece, ((0, tall - piece), (0, 0))),
        ],
        axis=1,
    )
    packed = lax.all_gather(pack, "dp", axis=0, tiled=False)
    w_qkv = attn_all[:, :shard, :cols].reshape(width, cols)
    wo = attn_all[:, :shard, cols:].reshape(H * HD, width)
    w_gate_up = packed[:, :shard, : 2 * ff_cols].reshape(width, 2 * ff_cols)
    wd = packed[:, :piece, 2 * ff_cols :].reshape(ff_cols, width)

    freqs = BASE ** (-(jnp.arange(HD // 2, dtype=F32) * (2.0 / HD)))
    freqs = jnp.concatenate([freqs] * 4)
    angles = jnp.arange(length, dtype=jnp.int32).astype(F32)[:, None] * freqs[None, :]

    normed, q_raw, k_raw, query, key, value, mixed, gains, cosine, sine, bounds = pl.pallas_call(
        functools.partial(forward_kernel, seqs),
        out_shape=(
            out(length, width, dtype=BF16),
            out(half, q_cols),
            out(length, kv_cols),
            out(half, q_cols, dtype=BF16),
            out(length, kv_cols, dtype=BF16),
            out(length, kv_cols, dtype=BF16),
            out(half, q_cols, dtype=BF16),
            out(16, width),
            out(length, 128),
            out(length, 128),
            out(8, 128),
        ),
        in_specs=[smem] + whole(seqs + 3),
        out_specs=tuple(whole(11)),
        scratch_shapes=[pltpu.VMEM((length, 128), BF16)] * 2,
        compiler_params=params,
        cost_estimate=pl.CostEstimate(
            flops=10_000_000_000, bytes_accessed=10_000_000, transcendentals=2_000_000
        ),
    )(me_ref, *token_parts, attn_all, jnp.cos(angles), jnp.sin(angles))
    attn_g = gains[0:1]
    ffn_g = gains[1:2]

    mixed = tie(mixed, *cot_parts)
    mixed_parts = scatter_side([mixed[k * rows : (k + 1) * rows] for k in range(SIDE)])
    attended_parts = jnp.stack(mixed_parts)
    attended = jnp.concatenate(
        [
            lax.dynamic_index_in_dim(attended_parts, side ^ j, axis=0, keepdims=False)
            for j in range(SIDE)
        ],
        axis=1,
    )
    states = tokens.astype(F32)
    resid = states + dot(attended, wo)
    normal2, inverse2 = norm_parts(resid)
    normed2 = (normal2 * ffn_g).astype(BF16)

    normed2_all = jnp.concatenate(gather_side(tie(normed2, w_qkv)), axis=0)
    attended_parts = gather_side(tie(attended, normed2_all))
    cot_all = jnp.concatenate(cot_parts, axis=0)
    gate_up = dot(normed2_all, w_gate_up)
    gate, upper = gate_up[:, :ff_cols], gate_up[:, ff_cols:]
    d_hidden = right_dot(cot_all, wd)
    sigmoid_gate = jax.nn.sigmoid(gate)
    active = gate * sigmoid_gate
    hidden = (active * upper).astype(BF16)
    d_gate = d_hidden * upper * sigmoid_gate * (1.0 + gate * (1.0 - sigmoid_gate))
    d_upper = d_hidden * active
    d_gate, d_upper = d_gate.astype(BF16), d_upper.astype(BF16)
    d_gate_up = jnp.concatenate([d_gate, d_upper], axis=1)
    d_normed2_part = right_dot(d_gate_up, w_gate_up).astype(BF16)

    def scatter_rows(blocks):
        return scatter_side([blocks[k * rows : (k + 1) * rows] for k in range(SIDE)])

    def sum_parts(received):
        return sum(part.astype(F32) for part in received)

    d_normed2_parts = scatter_rows(d_normed2_part)

    where = jnp.stack([me, core]).astype(jnp.int32)
    gate_up_keep, gate_up_send, down_part = pl.pallas_call(
        terms_kernel,
        out_shape=(
            out(dps // 2 * (shard + 32), 2 * ff_cols, dtype=BF16),
            out(dps // 2 * (shard + 32), 2 * ff_cols, dtype=BF16),
            out(half, width, dtype=BF16),
        ),
        in_specs=[smem] + whole(6),
        out_specs=tuple(whole(3)),
        scratch_shapes=[pltpu.VMEM((ff_cols, width), F32)],
        compiler_params=params,
        cost_estimate=pl.CostEstimate(
            flops=10_000_000_000, bytes_accessed=20_000_000, transcendentals=0
        ),
    )(
        where,
        normed2_all,
        tie(d_gate, d_normed2_part, *attended_parts),
        d_upper,
        hidden,
        cot_all,
        wd,
    )
    d_normed2_parts[0] = tie(d_normed2_parts[0], down_part)
    d_normed2 = sum_parts(d_normed2_parts)
    gate_up_got = swap(tie(gate_up_send, d_normed2), "dp", 1)

    d_resid = cot.astype(F32) + norm_back(d_normed2 * ffn_g, normal2, inverse2)
    d_resid_low = d_resid.astype(BF16)
    d_attended = right_dot(d_resid_low, wo).astype(BF16)
    out_cols = width // SIDE
    d_messages = scatter_side(
        [
            jnp.concatenate(
                [
                    lax.dynamic_slice_in_dim(d_attended, (side ^ k) * q_cols, q_cols, axis=1),
                    lax.dynamic_slice_in_dim(d_resid_low, (side ^ k) * out_cols, out_cols, axis=1),
                ],
                axis=1,
            )
            for k in range(SIDE)
        ]
    )
    gate_up_sum = added(gate_up_keep, tie(gate_up_got, d_attended))
    gate_up_parts = send_along_z(gate_up_sum.reshape(4, 2, shard + 32, -1), mine)
    down_parts = scatter_rows(tie(down_part, *d_messages))

    d_q_raw, d_kv_raw, attn_keep, attn_send = pl.pallas_call(
        backward_kernel,
        out_shape=(
            out(half, q_cols, dtype=BF16),
            out(length, 2 * kv_cols, dtype=BF16),
            out(width // 2, cols + out_cols + 128, dtype=BF16),
            out(width // 2, cols + out_cols + 128, dtype=BF16),
        ),
        in_specs=[smem] + whole(2 * SIDE + 10),
        out_specs=tuple(whole(4)),
        scratch_shapes=[
            pltpu.VMEM((length, 128), BF16),
            pltpu.VMEM((length, 128), BF16),
            pltpu.VMEM((2, length, 128), F32),
            pltpu.VMEM((2, length, 128), F32),
            pltpu.VMEM((half, q_cols), F32),
            pltpu.VMEM((half, q_cols), BF16),
            pltpu.VMEM((length, 128), F32),
            pltpu.VMEM((half, width), BF16),
            pltpu.VMEM((half, out_cols), BF16),
        ],
        compiler_params=params,
        cost_estimate=pl.CostEstimate(
            flops=14_000_000_000, bytes_accessed=10_000_000, transcendentals=2_000_000
        ),
    )(
        where,
        *d_messages,
        *attended_parts,
        query,
        key,
        value,
        q_raw,
        k_raw,
        cosine,
        sine,
        normed,
        gains,
        bounds,
    )
    gate_up_parts[0] = tie(gate_up_parts[0], d_kv_raw)
    gate_up_sum = added(*gate_up_parts)
    gate_up_got = swap(take(gate_up_sum, 1 - x, 0), "dp", 2)
    attn_got = swap(attn_send, "dp", 1)
    from_later = lax.ppermute(
        d_kv_raw[half:], "seq", [(i, i - SIDE) for i in range(SIDE, seqs)]
    )
    attn_sum = added(attn_keep, tie(attn_got, gate_up_sum))
    attn_parts = send_along_z(attn_sum.reshape(4, 2, shard, -1), mine)
    d_kv = added(d_kv_raw[:half], tie(from_later, attn_sum))
    d_qkv = jnp.concatenate([d_q_raw, d_kv], axis=1)
    d_normed_part = right_dot(d_qkv, w_qkv).astype(BF16)
    d_normed_parts = scatter_rows(d_normed_part)
    gate_up_share = added(take(gate_up_sum, x, 0), tie(gate_up_got, d_normed_part))
    gate_up_other = swap(gate_up_share, "seq", SIDE)
    attn_parts[0] = tie(attn_parts[0], gate_up_share)
    attn_sum = added(*attn_parts)
    attn_got = swap(take(attn_sum, 1 - x, 0), "dp", 2)
    down_parts[0] = tie(down_parts[0], attn_sum)
    block_out = (resid + sum_parts(down_parts)).astype(BF16)
    gate_up_share = added(gate_up_share, tie(gate_up_other, block_out))
    gate_up_parts = gather_side(gate_up_share)
    attn_share = added(take(attn_sum, x, 0), tie(attn_got, gate_up_share))
    attn_other = swap(attn_share, "seq", SIDE)
    attn_share = added(attn_share, attn_other)
    attn_parts = gather_side(attn_share)
    d_normed_parts[0] = tie(d_normed_parts[0], attn_share)
    d_normed = sum_parts(d_normed_parts)
    normal1, inverse1 = norm_parts(states)
    grad_inputs = d_resid + norm_back(d_normed * attn_g, normal1, inverse1)

    outs = pl.pallas_call(
        functools.partial(place_kernel, piece, dps),
        out_shape=(
            out(shard, H * HD),
            out(shard, KV * HD),
            out(shard, KV * HD),
            out(shard, width),
            out(shard, ff),
            out(shard, ff),
            out(SIDE * piece, width),
            out(shard, 128),
        ),
        in_specs=[smem] + whole(2 * SIDE + 5),
        out_specs=tuple(whole(8)),
        scratch_shapes=[
            pltpu.VMEM((SIDE,) + gate_up_share.shape, BF16),
            pltpu.VMEM((SIDE,) + attn_share.shape, BF16),
        ],
        compiler_params=params,
    )(
        side_ref,
        *gate_up_parts,
        *attn_parts,
        w_query,
        w_key,
        w_value,
        w_gate,
        w_up,
    )
    out_query, out_key, out_value, out_out, out_gate, out_up, out_down, out_gains = outs
    return (
        block_out[None],
        grad_inputs[None],
        out_query,
        out_key,
        out_value,
        out_out,
        out_gate,
        out_up,
        out_down,
        out_gains[:, 2] / attn_gain.astype(F32),
        out_gains[:, 3] / ffn_gain.astype(F32),
        out_gains[:few, 0],
        out_gains[:few, 1],
    )


def solution(mesh):
    tokens = P("dp", "seq", None)
    weight = P("dp", None)
    gain = P("dp")
    return jax.shard_map(
        shards,
        mesh=mesh,
        in_specs=(tokens, P("dp", "seq")) + (weight,) * 7 + (gain,) * 4 + (tokens,),
        out_specs=(tokens, tokens) + (weight,) * 7 + (gain,) * 4,
        check_vma=False,
    )
```
